32 devices in a mesh: grp: 2 (over y), row: 4 (over z), col: 2 (over x), sub: 2 (over core).
Axes of the slice: x: 2, y: 2, z: 4, core: 2. Of those that a mesh axis runs over, the one named last changes fastest.
Arguments:
- samples: bfloat16 [512, 2, 16, 512], P(('grp', 'row', 'col', 'sub')), parts along dimension 0, may hold values from -6 to 6
- analysis_taps: float32 [16, 16], replicated, may hold values from -1 to 1
- synthesis_taps: float32 [16, 16], replicated, may hold values from -1 to 1
- antenna_station: int32 [512], P('grp'), parts along dimension 0, may hold values from 0 to 31, as said below
- station_group: int32 [64, 1], P('grp'), parts along dimension 0, may hold values from 0 to 7
- beam_group: int32 [2048], P('grp'), parts along dimension 0, may hold values from 0 to 7
- beam_weights: bfloat16 [32, 2, 1024, 32], P(('grp', 'row'), None, ('col', 'sub')), parts along dimension 0, may hold values from -6 to 6
Outputs:
- visibilities: float32 [16, 2, 64, 32], P('row', None, ('grp', 'col', 'sub')), parts along dimension 2
- beam_series: float32 [2048, 2, 16, 512], P(('grp', 'col', 'sub', 'row')), parts along dimension 0
The draws below stay inside these ranges and needn't reach their ends.
There are 2 independent parts, one for each index of `grp`. The reference program is written for one: setup_inputs(seed, part) draws one part's arguments, and reference() takes and returns one part's arrays. A program takes and returns all parts, laid end to end along the dimension named above; an argument that names none is the same for every part. Nothing has to cross between parts.
Inputs may be any that keep to these rules, and one draw needn't show every extreme that they name: `antenna_station`: every station is named by exactly 8 antennas.
All inputs are finite; a program needn't handle non-finite values.
Results may differ from the reference program's by a relative error of at most 0.005.
Values may be sent and summed in bfloat16 or wider, within the bound.
A program may use at most 64 MiB of HBM per device.

```python
import math
import jax
import jax.numpy as jnp
from jax import lax

ANTENNAS = 256
ANTENNAS_PER_STN = 8
STATIONS = 32
CHAN = 16
TAPS = 16
SPEC = 512
BEAMS = 1024
GROUPS = 8


def draw_antenna_station(key, part):
    sort_order = jax.random.permutation(key, ANTENNAS)
    return (sort_order // ANTENNAS_PER_STN).astype(jnp.int32)


def plant(values, stream_key, low, largest):
    extent = values.shape
    spot = [jax.random.randint(jax.random.fold_in(stream_key, axis), (), 0, extent[axis]) for axis in range(len(extent))]
    values = values.at[tuple(spot)].set(low)
    longest = extent.index(max(extent))
    spot[longest] = (spot[longest] + 1) % extent[longest]
    return values.at[tuple(spot)].set(largest)


def levels(stream_key, shape, cuts, low, top_value):
    level, own = 1.0, jax.random.fold_in(stream_key, 6)
    for position, blocks in cuts:
        draws = jnp.exp(jax.random.uniform(jax.random.fold_in(own, position), (blocks,), jnp.float32, low / len(cuts), top_value / len(cuts)))
        level = level * jnp.repeat(draws, shape[position] // blocks).reshape([-1 if axis == position else 1 for axis in range(len(shape))])
    return level


def choose_distinct(key, rows, count, top, lift):
    sequence = jax.random.permutation(jax.random.fold_in(key, 1), count)
    favour = sequence
    for power in range(3):
        favour = favour * favour // count
    favour = favour * lift // count
    lots = jax.random.randint(jax.random.fold_in(key, 2), (rows, count), 0, 4096) + favour
    fixed_rows = jax.random.permutation(jax.random.fold_in(key, 3), rows)[jnp.arange(count) % rows]
    lots = jnp.where(jnp.arange(rows)[:, None] == fixed_rows[None, :], 1 << 14, lots)
    priority = lots * count + jnp.arange(count)
    return lax.top_k(priority.astype(jnp.int32), top)[1].astype(jnp.int32)


def normal_values(own_key, dims, width, limit, pieces=(), dtype=jnp.bfloat16):
    array = jax.random.normal(own_key, dims, jnp.float32) * width
    if len(pieces) > 0:
        array = levels(own_key, dims, pieces, -0.22, 0.18) * array
    return jnp.clip(array, min=-limit, max=limit).astype(dtype)


def setup_inputs(seed: int = 0, part: int = 0) -> dict:
    splits = jax.random.split(jax.random.key(seed), 8)
    part_splits = jax.random.split(jax.random.fold_in(splits[7], part), 8)
    return {
        "samples": normal_values(part_splits[0], (ANTENNAS, 2, CHAN, SPEC), 1.0, 6.0, ((0, 16),)),
        "analysis_taps": normal_values(splits[1], (TAPS, CHAN), 0.25, 1.0, (), jnp.float32),
        "synthesis_taps": normal_values(splits[2], (TAPS, CHAN), 0.25, 1.0, (), jnp.float32),
        "antenna_station": draw_antenna_station(jax.random.fold_in(jax.random.fold_in(splits[7], part), 71), part),
        "station_group": choose_distinct(part_splits[4], STATIONS, GROUPS, 1, 2048),
        "beam_group": plant(jax.random.randint(part_splits[5], (BEAMS,), 0, GROUPS), jax.random.fold_in(part_splits[5], 1), 0, GROUPS - 1).astype(jnp.int32),
        "beam_weights": normal_values(part_splits[6], (CHAN, 2, BEAMS, STATIONS), 1.0, 6.0, ((0, 4), (2, 4))),
    }


def polyphase(signal, coefficients):
    length = signal.shape[-1]
    output = coefficients[0][:, None] * signal
    for tap_index in range(1, coefficients.shape[0]):
        shifted = jnp.pad(signal[..., :length - tap_index], [(0, 0)] * (signal.ndim - 1) + [(tap_index, 0)])
        output = output + coefficients[tap_index][:, None] * shifted
    return output

def fourier_table(length, direction):
    indices = jnp.arange(length)
    angles = 2.0 * math.pi / length * (indices[:, None] * indices[None, :] % length).astype(jnp.float32)
    cosine_part = jnp.cos(angles)
    sine_part = jnp.sin(angles)
    table = jnp.stack([jnp.stack([cosine_part, direction * sine_part]), jnp.stack([-direction * sine_part, cosine_part])])
    return table.transpose(0, 2, 1, 3) * (1.0 / math.sqrt(length))

def reference(samples, analysis_taps, synthesis_taps, antenna_station, station_group, beam_group, beam_weights):
    filtered = polyphase(samples.astype(jnp.float32), analysis_taps)
    spectra = jnp.einsum('aqcf,qcpk->apkf', filtered, fourier_table(CHAN, -1.0), precision=lax.Precision.HIGHEST).astype(jnp.bfloat16)
    summed_values = jax.ops.segment_sum(spectra.astype(jnp.float32), antenna_station, num_segments=STATIONS)
    station_list = (summed_values * (1.0 / math.sqrt(ANTENNAS_PER_STN))).astype(jnp.bfloat16)
    real_part = station_list[:, 0].astype(jnp.float32)
    imag_part = station_list[:, 1].astype(jnp.float32)
    high = lax.Precision.HIGHEST
    vis_real = (jnp.einsum('icf,jcf->cij', real_part, real_part, precision=high) + jnp.einsum('icf,jcf->cij', imag_part, imag_part, precision=high)) * (1.0 / SPEC)
    vis_imag = (jnp.einsum('icf,jcf->cij', imag_part, real_part, precision=high) - jnp.einsum('icf,jcf->cij', real_part, imag_part, precision=high)) * (1.0 / SPEC)
    visibilities = jnp.stack([vis_real, vis_imag], axis=1)
    members = station_group[:, 0][None, :] == beam_group[:, None]
    scaling = 1.0 / jnp.sqrt(lax.optimization_barrier(jnp.sum(members.astype(jnp.float32), axis=1)))
    weights = jnp.where(members[None, None], beam_weights, jnp.zeros((), jnp.bfloat16)).astype(jnp.float32)
    weight_real = weights[:, 0]
    imaginary_weight = weights[:, 1]
    beam_real = jnp.einsum('cbs,scf->bcf', weight_real, real_part, precision=high) - jnp.einsum('cbs,scf->bcf', imaginary_weight, imag_part, precision=high)
    beam_imag = jnp.einsum('cbs,scf->bcf', weight_real, imag_part, precision=high) + jnp.einsum('cbs,scf->bcf', imaginary_weight, real_part, precision=high)
    beams = (jnp.stack([beam_real, beam_imag], axis=1) * scaling[:, None, None, None]).astype(jnp.bfloat16)
    inverse = jnp.einsum('bqkf,qkpc->bpcf', beams.astype(jnp.float32), fourier_table(CHAN, 1.0), precision=high)
    beam_series = polyphase(inverse, synthesis_taps)
    return (visibilities, beam_series)
```

```python
import functools
import math

import jax
import jax.numpy as jnp
import numpy as np
from jax import lax
from jax.experimental import pallas as pl
from jax.experimental.pallas import tpu as pltpu
from jax.sharding import PartitionSpec as P

MESH = pl.DeviceIdType.MESH

ANTENNAS_PER_STN = 8
SPEC = 512


def polyphase(signal, coefficients):
    length = signal.shape[-1]
    output = coefficients[0][:, None] * signal
    for tap_index in range(1, coefficients.shape[0]):
        shifted = jnp.pad(
            signal[..., : length - tap_index], [(0, 0)] * (signal.ndim - 1) + [(tap_index, 0)]
        )
        output = output + coefficients[tap_index][:, None] * shifted
    return output


def fourier_table(length, direction):
    indices = jnp.arange(length)
    angles = (
        2.0 * math.pi / length * (indices[:, None] * indices[None, :] % length).astype(jnp.float32)
    )
    cosine_part = jnp.cos(angles)
    sine_part = jnp.sin(angles)
    table = jnp.stack(
        [
            jnp.stack([cosine_part, direction * sine_part]),
            jnp.stack([-direction * sine_part, cosine_part]),
        ]
    )
    return table.transpose(0, 2, 1, 3) * (1.0 / math.sqrt(length))


def body(
    samples, analysis_taps, synthesis_taps, antenna_station, station_group, beam_group, beam_weights
):
    high = lax.Precision.HIGHEST
    block_count = lax.axis_size(("col", "sub"))
    block_index = lax.axis_index(("col", "sub"))
    filtered = polyphase(samples.astype(jnp.float32), analysis_taps)
    spectra = jnp.einsum(
        "aqcf,qcpk->apkf", filtered, fourier_table(samples.shape[2], -1.0), precision=high
    ).astype(jnp.bfloat16)
    turned = lax.all_to_all(spectra, "row", split_axis=2, concat_axis=0, tiled=True)
    local_count = spectra.shape[0]
    held_rows = turned.shape[0]
    chan_rows = turned.shape[2]
    spec_len = turned.shape[3]
    station_count = station_group.shape[0]
    flat_width = 2 * chan_rows * spec_len
    tile_rows = station_count // block_count
    shard_rows = lax.all_gather(turned, ("col", "sub"), axis=0, tiled=True)
    row_total = shard_rows.shape[0]
    positions = jnp.arange(row_total, dtype=jnp.int32)
    source_block = positions // held_rows
    offset_rows = positions % held_rows
    source_row = offset_rows // local_count
    antenna = offset_rows % local_count
    global_index = (source_row * block_count + source_block) * local_count + antenna
    targets = antenna_station[global_index]
    wanted = jnp.arange(station_count, dtype=jnp.int32)
    one_hot = (targets[None, :] == wanted[:, None]).astype(jnp.bfloat16)
    summed_values = jnp.dot(
        one_hot, shard_rows.reshape(row_total, flat_width), preferred_element_type=jnp.float32
    )
    flat_stations = (summed_values * (1.0 / math.sqrt(ANTENNAS_PER_STN))).astype(jnp.bfloat16)
    station_list = flat_stations.reshape(station_count, 2, chan_rows, spec_len)
    real_part = station_list[:, 0]
    imag_part = station_list[:, 1]
    own_rows = lax.dynamic_slice_in_dim(station_list, block_index * tile_rows, tile_rows, 0)
    own_real = own_rows[:, 0]
    own_imag = own_rows[:, 1]
    vis_real = (
        jnp.einsum("icf,jcf->cij", own_real, real_part, preferred_element_type=jnp.float32)
        + jnp.einsum("icf,jcf->cij", own_imag, imag_part, preferred_element_type=jnp.float32)
    ) * (1.0 / SPEC)
    vis_imag = (
        jnp.einsum("icf,jcf->cij", own_imag, real_part, preferred_element_type=jnp.float32)
        - jnp.einsum("icf,jcf->cij", own_real, imag_part, preferred_element_type=jnp.float32)
    ) * (1.0 / SPEC)
    visibilities = jnp.stack([vis_real, vis_imag], axis=1)
    beam_block = beam_weights.shape[2]
    own_groups = lax.dynamic_slice_in_dim(beam_group, block_index * beam_block, beam_block, 0)
    members = station_group[:, 0][None, :] == own_groups[:, None]
    scaling = 1.0 / jnp.sqrt(jnp.sum(members.astype(jnp.float32), axis=1))
    weights = jnp.where(members[None, None], beam_weights, jnp.zeros((), jnp.bfloat16))
    weight_real = weights[:, 0]
    imaginary_weight = weights[:, 1]
    beam_real = jnp.einsum(
        "cbs,scf->bcf", weight_real, real_part, preferred_element_type=jnp.float32
    ) - jnp.einsum("cbs,scf->bcf", imaginary_weight, imag_part, preferred_element_type=jnp.float32)
    beam_imag = jnp.einsum(
        "cbs,scf->bcf", weight_real, imag_part, preferred_element_type=jnp.float32
    ) + jnp.einsum("cbs,scf->bcf", imaginary_weight, real_part, preferred_element_type=jnp.float32)
    beams = (jnp.stack([beam_real, beam_imag], axis=1) * scaling[:, None, None, None]).astype(
        jnp.bfloat16
    )
    returned = lax.all_to_all(beams, "row", split_axis=0, concat_axis=2, tiled=True)
    inverse = jnp.einsum(
        "bqkf,qkpc->bpcf",
        returned.astype(jnp.float32),
        fourier_table(returned.shape[2], 1.0),
        precision=high,
    )
    beam_series = polyphase(inverse, synthesis_taps)
    return (visibilities, beam_series)


def exchange_kernel(
    n_row, n_col, n_sub,
    x_ref, w_ref, station_ref, taps_ref,
    lanes_ref, w_out_ref,
    recv, own_sem, send_sem, recv_sem, w_send, w_recv, g_send, g_recv,
):
    n = n_row * n_col * n_sub
    row, col, sub = lax.axis_index("row"), lax.axis_index("col"), lax.axis_index("sub")
    me = (row * n_col + col) * n_sub + sub

    def coords(index):
        return {
            "row": lax.div(index, n_col * n_sub),
            "col": lax.rem(lax.div(index, n_sub), n_col),
            "sub": lax.rem(index, n_sub),
        }

    barrier = pltpu.get_barrier_semaphore()

    def greet(step, carry):
        pl.semaphore_signal(
            barrier, inc=1, device_id=coords(lax.rem(me + step, n)), device_id_type=MESH
        )
        return carry

    lax.fori_loop(1, n, greet, 0)
    own = pltpu.make_async_copy(x_ref.at[me], recv.at[me], own_sem.at[0])
    own.start()
    own_w = pltpu.make_async_copy(w_ref.at[row], w_out_ref.at[row], own_sem.at[1])
    own_w.start()
    pl.semaphore_wait(barrier, n - 1)

    def slab(step):
        peer = lax.rem(me + step, n)
        return pltpu.make_async_remote_copy(
            src_ref=x_ref.at[peer], dst_ref=recv.at[me],
            send_sem=send_sem.at[step], recv_sem=recv_sem.at[step],
            device_id=coords(peer), device_id_type=MESH,
        )

    def weight(step):
        peer = lax.rem(row + step, n_row)
        return pltpu.make_async_remote_copy(
            src_ref=w_ref.at[peer], dst_ref=w_out_ref.at[row],
            send_sem=w_send.at[step], recv_sem=w_recv.at[step],
            device_id={"row": peer, "col": col, "sub": sub}, device_id_type=MESH,
        )

    def start_slab(step, carry):
        slab(step).start()
        return carry

    lax.fori_loop(1, n, start_slab, 0)
    for step in range(1, n_row):
        weight(step).start()

    stations2, width = lanes_ref.shape[1], lanes_ref.shape[2]
    stations = stations2 // 2
    per = x_ref.shape[1]
    total = n * per
    place = lax.broadcasted_iota(jnp.int32, (stations2, total), 0)
    column = lax.broadcasted_iota(jnp.int32, (stations2, total), 1)
    part = lax.rem(lax.div(column, per // 2), 2)
    wanted = station_ref[...] + part * stations
    one_hot = jnp.where(place == wanted, 1.0, 0.0).astype(jnp.bfloat16)

    own.wait()

    def finish_slab(step, carry):
        slab(step).wait_recv()
        return carry

    lax.fori_loop(1, n, finish_slab, 0)
    summed = jnp.dot(
        one_hot, recv[...].reshape(total, width), preferred_element_type=jnp.float32
    )
    frame = lax.broadcasted_iota(jnp.int32, summed.shape, 1)
    filtered = taps_ref[0, me] * summed
    for tap in range(1, taps_ref.shape[0]):
        moved = jnp.where(frame >= tap, pltpu.roll(summed, tap, 1), 0.0)
        filtered = filtered + taps_ref[tap, me] * moved
    scale = 1.0 / math.sqrt(ANTENNAS_PER_STN * n)
    lanes_ref[me] = (filtered * scale).astype(jnp.bfloat16)

    def forward(lane, slot, target):
        return pltpu.make_async_remote_copy(
            src_ref=lanes_ref.at[lane], dst_ref=lanes_ref.at[lane],
            send_sem=g_send.at[slot], recv_sem=g_recv.at[lane],
            device_id=target, device_id_type=MESH,
        )

    def lane_of(r, c, s):
        return (r * n_col + c) * n_sub + s

    other_col = {"row": row, "col": 1 - col, "sub": sub}
    other_sub = {"row": row, "col": col, "sub": 1 - sub}
    sends = []

    def send(lane, target):
        copy = forward(lane, len(sends), target)
        copy.start()
        sends.append(copy)

    def arrived(lane):
        forward(lane, 0, other_sub).wait_recv()

    for step in range(1, n_row):
        send(me, {"row": lax.rem(row + step, n_row), "col": col, "sub": sub})
    send(me, other_col)
    send(me, other_sub)
    for step in range(1, n_row):
        lane = lane_of(lax.rem(row + n_row - step, n_row), col, sub)
        arrived(lane)
        send(lane, other_col)
        send(lane, other_sub)
    for step in range(n_row):
        lane = lane_of(lax.rem(row + n_row - step, n_row), 1 - col, sub)
        arrived(lane)
        send(lane, other_sub)
    for step in range(n_row):
        for c in range(n_col):
            arrived(lane_of(lax.rem(row + n_row - step, n_row), c, 1 - sub))
    for copy in sends:
        copy.wait_send()

    def finish_send(step, carry):
        slab(step).wait_send()
        return carry

    lax.fori_loop(1, n, finish_send, 0)
    own_w.wait()
    for step in range(1, n_row):
        weight(step).wait()


def exchange(x, w, station_row, taps, n_row, n_col, n_sub):
    n = n_row * n_col * n_sub
    stations2 = station_row[1]
    any_space = pl.BlockSpec(memory_space=pl.ANY)
    vmem = pl.BlockSpec(memory_space=pltpu.VMEM)
    width = x.shape[2]
    dma = pltpu.SemaphoreType.DMA
    sends = (n_row - 1) * 3 + 2 + n_row
    return pl.pallas_call(
        functools.partial(exchange_kernel, n_row, n_col, n_sub),
        out_shape=(
            jax.ShapeDtypeStruct((n, stations2, width), jnp.bfloat16),
            jax.ShapeDtypeStruct(w.shape, jnp.bfloat16),
        ),
        in_specs=[any_space, any_space, vmem, pl.BlockSpec(memory_space=pltpu.SMEM)],
        out_specs=(vmem, vmem),
        scratch_shapes=[
            pltpu.VMEM((n, x.shape[1], width), jnp.bfloat16),
            dma((2,)), dma((n,)), dma((n,)), dma((n_row,)), dma((n_row,)),
            dma((sends,)), dma((n,)),
        ],
        compiler_params=pltpu.CompilerParams(
            collective_id=0, has_side_effects=True, vmem_limit_bytes=32 * 1024 * 1024
        ),
        name="exchange",
    )(x, w, station_row[0], taps)


def fourier(points):
    count = len(points)
    if count == 1:
        return points
    even, odd = fourier(points[0::2]), fourier(points[1::2])
    half = count // 2
    low, high = [], []
    for index in range(half):
        (er, ei), (r, i) = even[index], odd[index]
        if index == 0:
            tr, ti = r, i
        elif 4 * index == count:
            tr, ti = i, -r
        else:
            c, s = math.cos(2 * math.pi * index / count), math.sin(2 * math.pi * index / count)
            if 8 * index == count:
                tr, ti = (r + i) * c, (i - r) * c
            elif 8 * index == 3 * count:
                tr, ti = (i - r) * s, -(r + i) * s
            else:
                tr, ti = r * c + i * s, i * c - r * s
        low.append((er + tr, ei + ti))
        high.append((er - tr, ei - ti))
    return low + high


def beam_kernel(
    lanes_ref, w_ref, sgroup_ref, bgroup_ref, cos_ref, sin_ref, taps_ref,
    vis_ref, out_ref, spectra, gram, inverse,
):
    chan, stations2, width = lanes_ref.shape
    stations = stations2 // 2

    @pl.when(pl.program_id(0) == 0)
    def _():
        step_rows = 16

        @pl.loop(0, stations // step_rows)
        def _(block):
            low = pl.multiple_of(block * step_rows, step_rows)
            for start in range(0, width, 128):
                points = [
                    (
                        lanes_ref[c, pl.ds(low, step_rows), start : start + 128].astype(jnp.float32),
                        lanes_ref[c, pl.ds(low + stations, step_rows), start : start + 128].astype(
                            jnp.float32
                        ),
                    )
                    for c in range(chan)
                ]
                for k, (re, im) in enumerate(fourier(points)):
                    spectra[k, pl.ds(low, step_rows), start : start + 128] = re.astype(jnp.bfloat16)
                    spectra[k, pl.ds(low + stations, step_rows), start : start + 128] = im.astype(
                        jnp.bfloat16
                    )

        chan_rows, _, own, _ = vis_ref.shape
        first = lax.axis_index("row") * chan_rows
        block_index = lax.axis_index(("col", "sub"))
        begin = pl.multiple_of(block_index * own, own)
        for k in range(chan_rows):
            block = spectra[first + k]
            gram[...] = lax.dot_general(
                block, block, (((1,), (1,)), ((), ())), preferred_element_type=jnp.float32
            )
            top = gram[pl.ds(begin, own), :]
            bottom = gram[pl.ds(begin + stations, own), :]
            vis_ref[k, 0] = (top[:, :stations] + bottom[:, stations:]) * (1.0 / width)
            vis_ref[k, 1] = (bottom[:, :stations] - top[:, stations:]) * (1.0 / width)

    rows = bgroup_ref.shape[0]
    total = chan * stations2
    weight = jnp.concatenate([w_ref[r] for r in range(w_ref.shape[0])], axis=1).astype(jnp.float32)
    members = sgroup_ref[...] == bgroup_ref[...]
    count = jnp.sum(members.astype(jnp.float32), axis=1, keepdims=True) * (1.0 / (2 * chan))
    weight = jnp.where(members, weight, 0.0) * (1.0 / jnp.sqrt(count))
    position = lax.broadcasted_iota(jnp.int32, (rows, total), 1)
    first_half = lax.rem(position, stations2) < stations
    plain = jnp.where(first_half, weight, -weight)
    swapped = jnp.where(
        first_half, pltpu.roll(weight, total - stations, 1), pltpu.roll(weight, stations, 1)
    )
    cos_table, sin_table = cos_ref[...], sin_ref[...]
    matrix = []
    for b in range(rows):
        a0, a1 = plain[b : b + 1], swapped[b : b + 1]
        matrix.append((cos_table * a0 - sin_table * a1).astype(jnp.bfloat16))
        matrix.append((cos_table * a1 + sin_table * a0).astype(jnp.bfloat16))
    inverse[...] = jnp.dot(
        jnp.concatenate(matrix, axis=0),
        spectra[...].reshape(total, width),
        preferred_element_type=jnp.float32,
    )
    lane = lax.broadcasted_iota(jnp.int32, (chan, 128), 1)

    def shift(tiles, amount):
        turned = [pltpu.roll(tile, amount, 1) for tile in tiles]
        before = [jnp.zeros_like(turned[0])] + turned[:-1]
        return [jnp.where(lane >= amount, t, b) for t, b in zip(turned, before)]

    taps = taps_ref.shape[0]
    stride = 4
    for index in range(2 * rows):
        tiles = [
            inverse[index * chan : (index + 1) * chan, start : start + 128]
            for start in range(0, width, 128)
        ]
        moved = [tiles]
        for amount in range(1, stride):
            moved.append(shift(tiles, amount))
        total_tiles = None
        for high in range(taps // stride - 1, -1, -1):
            if total_tiles is not None:
                total_tiles = shift(total_tiles, stride)
            for low in range(stride):
                tap = taps_ref[high * stride + low]
                terms = [tap * tile for tile in moved[low]]
                total_tiles = (
                    terms if total_tiles is None else [a + t for a, t in zip(total_tiles, terms)]
                )
        for number, tile in enumerate(total_tiles):
            out_ref[index // 2, index % 2, :, number * 128 : (number + 1) * 128] = tile


def beamform(lanes, w, sgroup, bgroup, cos_table, sin_table, taps, vis_shape, rows):
    chan, stations2, width = lanes.shape
    beams = bgroup.shape[0]
    whole = lambda *shape: pl.BlockSpec(shape, lambda i: (0,) * len(shape))
    return pl.pallas_call(
        beam_kernel,
        grid=(beams // rows,),
        out_shape=(
            jax.ShapeDtypeStruct(vis_shape, jnp.float32),
            jax.ShapeDtypeStruct((beams, 2, chan, width), jnp.float32),
        ),
        in_specs=[
            whole(*lanes.shape),
            pl.BlockSpec((w.shape[0], rows, w.shape[2]), lambda i: (0, i, 0)),
            whole(*sgroup.shape),
            pl.BlockSpec((rows, 1), lambda i: (i, 0)),
            whole(*cos_table.shape),
            whole(*sin_table.shape),
            whole(*taps.shape),
        ],
        out_specs=(
            whole(*vis_shape),
            pl.BlockSpec((rows, 2, chan, width), lambda i: (i, 0, 0, 0)),
        ),
        scratch_shapes=[
            pltpu.VMEM((chan, stations2, width), jnp.bfloat16),
            pltpu.VMEM((stations2, stations2), jnp.float32),
            pltpu.VMEM((rows * 2 * chan, width), jnp.float32),
        ],
        compiler_params=pltpu.CompilerParams(
            dimension_semantics=("arbitrary",), vmem_limit_bytes=40 * 1024 * 1024
        ),
        name="beamform",
    )(lanes, w, sgroup, bgroup, cos_table, sin_table, taps)


def lane_body(
    samples, analysis_taps, synthesis_taps, antenna_station, station_group, beam_group, beam_weights
):
    n_row, n_col, n_sub = (lax.axis_size(name) for name in ("row", "col", "sub"))
    local, _, chan, width = samples.shape
    n = n_row * n_col * n_sub
    stations = station_group.shape[0]
    x = samples.transpose(2, 1, 0, 3).reshape(chan, 2 * local, width)
    chan_rows, _, block, _ = beam_weights.shape
    beams = block // n_row
    w = (
        beam_weights.reshape(chan_rows, 2, n_row, beams, stations)
        .transpose(2, 3, 0, 1, 4)
        .reshape(n_row, beams, chan_rows * 2 * stations)
    )
    station_row = jnp.broadcast_to(antenna_station.reshape(n, 1, local), (n, 2, local)).reshape(1, -1)
    lanes, w_all = exchange(
        x, w, (station_row, 2 * stations), analysis_taps, n_row, n_col, n_sub
    )
    index = lax.axis_index(("col", "sub", "row"))
    bgroup = lax.dynamic_slice_in_dim(beam_group, index * beams, beams, 0)[:, None]
    sgroup = jnp.tile(station_group[:, 0], 2 * chan)[None, :]
    angle = 2.0 * np.pi / chan * (np.arange(chan)[:, None] * np.arange(chan)[None, :] % chan)
    spread = lambda t: jnp.asarray(
        np.repeat(t / math.sqrt(chan), 2 * stations, axis=1).astype(np.float32)
    )
    taps = jnp.broadcast_to(synthesis_taps[:, :, None], synthesis_taps.shape + (128,))
    tile_rows = stations // (n_col * n_sub)
    vis, series = beamform(
        lanes, w_all, sgroup, bgroup, spread(np.cos(angle)), spread(np.sin(angle)), taps,
        (chan_rows, 2, tile_rows, stations), 8,
    )
    return vis, series


def solution(mesh):
    shape = mesh.shape
    fits = (
        shape["row"] * shape["col"] * shape["sub"] == 16 and shape["col"] == 2 and shape["sub"] == 2
    )
    return jax.shard_map(
        lane_body if fits else body,
        mesh=mesh,
        in_specs=(
            P(("grp", "row", "col", "sub"), None, None, None),
            P(),
            P(),
            P("grp"),
            P("grp", None),
            P("grp"),
            P(("grp", "row"), None, ("col", "sub"), None),
        ),
        out_specs=(
            P("row", None, ("grp", "col", "sub"), None),
            P(("grp", "col", "sub", "row"), None, None, None),
        ),
        check_vma=False,
    )
```

```python
import functools
import math

import jax
import jax.numpy as jnp
from jax import lax
from jax.experimental import pallas as pl
from jax.experimental.pallas import tpu as pltpu
from jax.sharding import PartitionSpec as P

MESH = pl.DeviceIdType.MESH

ANTENNAS_PER_STN = 8
SPEC = 512


def polyphase(signal, coefficients):
    length = signal.shape[-1]
    output = coefficients[0][:, None] * signal
    for tap_index in range(1, coefficients.shape[0]):
        shifted = jnp.pad(
            signal[..., : length - tap_index], [(0, 0)] * (signal.ndim - 1) + [(tap_index, 0)]
        )
        output = output + coefficients[tap_index][:, None] * shifted
    return output


def fourier_table(length, direction):
    indices = jnp.arange(length)
    angles = (
        2.0 * math.pi / length * (indices[:, None] * indices[None, :] % length).astype(jnp.float32)
    )
    cosine_part = jnp.cos(angles)
    sine_part = jnp.sin(angles)
    table = jnp.stack(
        [
            jnp.stack([cosine_part, direction * sine_part]),
            jnp.stack([-direction * sine_part, cosine_part]),
        ]
    )
    return table.transpose(0, 2, 1, 3) * (1.0 / math.sqrt(length))


def body(
    samples, analysis_taps, synthesis_taps, antenna_station, station_group, beam_group, beam_weights
):
    high = lax.Precision.HIGHEST
    block_count = lax.axis_size(("col", "sub"))
    block_index = lax.axis_index(("col", "sub"))
    filtered = polyphase(samples.astype(jnp.float32), analysis_taps)
    spectra = jnp.einsum(
        "aqcf,qcpk->apkf", filtered, fourier_table(samples.shape[2], -1.0), precision=high
    ).astype(jnp.bfloat16)
    turned = lax.all_to_all(spectra, "row", split_axis=2, concat_axis=0, tiled=True)
    local_count = spectra.shape[0]
    held_rows = turned.shape[0]
    chan_rows = turned.shape[2]
    spec_len = turned.shape[3]
    station_count = station_group.shape[0]
    flat_width = 2 * chan_rows * spec_len
    tile_rows = station_count // block_count
    shard_rows = lax.all_gather(turned, ("col", "sub"), axis=0, tiled=True)
    row_total = shard_rows.shape[0]
    positions = jnp.arange(row_total, dtype=jnp.int32)
    source_block = positions // held_rows
    offset_rows = positions % held_rows
    source_row = offset_rows // local_count
    antenna = offset_rows % local_count
    global_index = (source_row * block_count + source_block) * local_count + antenna
    targets = antenna_station[global_index]
    wanted = jnp.arange(station_count, dtype=jnp.int32)
    one_hot = (targets[None, :] == wanted[:, None]).astype(jnp.bfloat16)
    summed_values = jnp.dot(
        one_hot, shard_rows.reshape(row_total, flat_width), preferred_element_type=jnp.float32
    )
    flat_stations = (summed_values * (1.0 / math.sqrt(ANTENNAS_PER_STN))).astype(jnp.bfloat16)
    station_list = flat_stations.reshape(station_count, 2, chan_rows, spec_len)
    real_part = station_list[:, 0]
    imag_part = station_list[:, 1]
    own_rows = lax.dynamic_slice_in_dim(station_list, block_index * tile_rows, tile_rows, 0)
    own_real = own_rows[:, 0]
    own_imag = own_rows[:, 1]
    vis_real = (
        jnp.einsum("icf,jcf->cij", own_real, real_part, preferred_element_type=jnp.float32)
        + jnp.einsum("icf,jcf->cij", own_imag, imag_part, preferred_element_type=jnp.float32)
    ) * (1.0 / SPEC)
    vis_imag = (
        jnp.einsum("icf,jcf->cij", own_imag, real_part, preferred_element_type=jnp.float32)
        - jnp.einsum("icf,jcf->cij", own_real, imag_part, preferred_element_type=jnp.float32)
    ) * (1.0 / SPEC)
    visibilities = jnp.stack([vis_real, vis_imag], axis=1)
    beam_block = beam_weights.shape[2]
    own_groups = lax.dynamic_slice_in_dim(beam_group, block_index * beam_block, beam_block, 0)
    members = station_group[:, 0][None, :] == own_groups[:, None]
    scaling = 1.0 / jnp.sqrt(jnp.sum(members.astype(jnp.float32), axis=1))
    weights = jnp.where(members[None, None], beam_weights, jnp.zeros((), jnp.bfloat16))
    weight_real = weights[:, 0]
    imaginary_weight = weights[:, 1]
    beam_real = jnp.einsum(
        "cbs,scf->bcf", weight_real, real_part, preferred_element_type=jnp.float32
    ) - jnp.einsum("cbs,scf->bcf", imaginary_weight, imag_part, preferred_element_type=jnp.float32)
    beam_imag = jnp.einsum(
        "cbs,scf->bcf", weight_real, imag_part, preferred_element_type=jnp.float32
    ) + jnp.einsum("cbs,scf->bcf", imaginary_weight, real_part, preferred_element_type=jnp.float32)
    beams = (jnp.stack([beam_real, beam_imag], axis=1) * scaling[:, None, None, None]).astype(
        jnp.bfloat16
    )
    returned = lax.all_to_all(beams, "row", split_axis=0, concat_axis=2, tiled=True)
    inverse = jnp.einsum(
        "bqkf,qkpc->bpcf",
        returned.astype(jnp.float32),
        fourier_table(returned.shape[2], 1.0),
        precision=high,
    )
    beam_series = polyphase(inverse, synthesis_taps)
    return (visibilities, beam_series)


def exchange_kernel(
    n_row, n_col, n_sub,
    samples_hbm, w_hbm, station_hbm, taps_hbm, sgroup_hbm, bgroup_hbm,
    lanes_ref, matrix_ref,
    samples_ref, w_ref, station_ref, taps_ref, sgroup_ref, bgroup_ref,
    x_ref, recv, w_mine, w_all, plain_ref, swapped_ref,
    load_sem, own_sem, send_sem, recv_sem, w_send, w_recv, g_send, g_recv,
):
    n = n_row * n_col * n_sub
    row, col, sub = lax.axis_index("row"), lax.axis_index("col"), lax.axis_index("sub")
    me = (row * n_col + col) * n_sub + sub
    halves, _, stations2, width = lanes_ref.shape
    stations = stations2 // 2
    local = samples_ref.shape[0]
    chan = n
    f32, bf16 = jnp.float32, jnp.bfloat16

    def coords(index):
        return {
            "row": lax.div(index, n_col * n_sub),
            "col": lax.rem(lax.div(index, n_sub), n_col),
            "sub": lax.rem(index, n_sub),
        }

    barrier = pltpu.get_barrier_semaphore()

    def greet(step, carry):
        pl.semaphore_signal(
            barrier, inc=1, device_id=coords(lax.rem(me + step, n)), device_id_type=MESH
        )
        return carry

    lax.fori_loop(1, n, greet, 0)
    pairs = [
        (samples_hbm, samples_ref), (w_hbm, w_ref), (station_hbm, station_ref),
        (taps_hbm, taps_ref), (sgroup_hbm, sgroup_ref), (bgroup_hbm, bgroup_ref),
    ]
    loads = [pltpu.make_async_copy(a, b, load_sem.at[i]) for i, (a, b) in enumerate(pairs)]
    for load in loads:
        load.start()

    total = local * 2 * chan
    block = 128
    loads[0].wait()
    source = samples_ref[...].reshape(total, halves * width)
    for start in range(0, total, block):
        to = lax.broadcasted_iota(jnp.int32, (block, total), 0) + start
        origin = lax.broadcasted_iota(jnp.int32, (block, total), 1)
        wanted = (
            lax.rem(to, local) * (2 * chan)
            + lax.rem(lax.div(to, local), 2) * chan
            + lax.div(to, 2 * local)
        )
        turn = jnp.where(origin == wanted, 1.0, 0.0).astype(bf16)
        turned = jnp.dot(turn, source, preferred_element_type=f32).astype(bf16)
        lanes_here = block // (2 * local)
        first = start // (2 * local)
        for h in range(halves):
            x_ref[first : first + lanes_here, h] = turned[:, h * width : (h + 1) * width].reshape(
                lanes_here, 2, local, width
            )
    for load in loads[1:]:
        load.wait()
    beams = w_mine.shape[1]
    flipped = w_ref[...].astype(f32).T.astype(bf16)
    for r in range(n_row):
        w_mine[r] = flipped[r * beams : (r + 1) * beams]
    for h in range(halves):
        recv[h, :, me] = x_ref[me, h]
    w_all[row] = w_mine[row]

    pl.semaphore_wait(barrier, n - 1)

    def slab(h, step):
        peer = lax.rem(me + step, n)
        return pltpu.make_async_remote_copy(
            src_ref=x_ref.at[peer, h], dst_ref=recv.at[h, :, me],
            send_sem=send_sem.at[h, step], recv_sem=recv_sem.at[h, step],
            device_id=coords(peer), device_id_type=MESH,
        )

    def weight(step):
        peer = lax.rem(row + step, n_row)
        return pltpu.make_async_remote_copy(
            src_ref=w_mine.at[peer], dst_ref=w_all.at[row],
            send_sem=w_send.at[step], recv_sem=w_recv.at[step],
            device_id={"row": peer, "col": col, "sub": sub}, device_id_type=MESH,
        )

    for step in range(1, n_row):
        weight(step).start()
    for h in range(halves):

        def start_slab(step, carry, h=h):
            slab(h, step).start()
            return carry

        lax.fori_loop(1, n, start_slab, 0)

    def column(values, offset, size):
        there = lax.broadcasted_iota(jnp.int32, (size, values.shape[1]), 1)
        here = lax.broadcasted_iota(jnp.int32, (size, values.shape[1]), 0) + offset
        return jnp.sum(jnp.where(there == here, values, 0.0), axis=1, keepdims=True)

    across = bgroup_ref.shape[1]
    begin = ((col * n_sub + sub) * n_row + row) * beams
    own_groups = column(
        bgroup_ref[pl.ds(lax.div(begin, across), 1), :].astype(f32), lax.rem(begin, across), beams
    )
    groups = sgroup_ref[...].astype(f32)
    members = jnp.where(groups == own_groups, 1.0, 0.0)
    scaling = 1.0 / jnp.sqrt(jnp.sum(members, axis=1, keepdims=True))
    mask = jnp.concatenate([members] * (128 // stations), axis=1)
    mask = jnp.concatenate([mask] * (chan * stations2 // 128), axis=1)
    for step in range(1, n_row):
        weight(step).wait_recv()
    columns = chan * stations2
    weights = jnp.concatenate([w_all[r] for r in range(n_row)], axis=1).astype(f32)
    weights = jnp.where(mask > 0.5, weights, 0.0) * scaling
    position = lax.broadcasted_iota(jnp.int32, (beams, columns), 1)
    first_half = lax.rem(position, stations2) < stations
    plain_ref[...] = jnp.where(first_half, weights, -weights)
    swapped_ref[...] = jnp.where(
        first_half, pltpu.roll(weights, columns - stations, 1), pltpu.roll(weights, stations, 1)
    )
    turn_index = lax.rem(
        lax.broadcasted_iota(jnp.int32, (chan, columns), 0)
        * lax.div(lax.broadcasted_iota(jnp.int32, (chan, columns), 1), stations2),
        chan,
    )
    cos_table = jnp.zeros((chan, columns), f32)
    sin_table = jnp.zeros((chan, columns), f32)
    for m in range(chan):
        angle = 2 * math.pi * m / chan
        hit = turn_index == m
        cos_table = jnp.where(hit, math.cos(angle) / math.sqrt(chan), cos_table)
        sin_table = jnp.where(hit, math.sin(angle) / math.sqrt(chan), sin_table)

    def fill(index, carry):
        low = pl.multiple_of(index * 8, 8)
        plain, swapped = plain_ref[pl.ds(low, 8), :], swapped_ref[pl.ds(low, 8), :]
        for b in range(8):
            a0, a1 = plain[b : b + 1], swapped[b : b + 1]
            at = pl.multiple_of((low + b) * 2 * chan, 2 * chan)
            matrix_ref[pl.ds(at, chan), :] = (cos_table * a0 - sin_table * a1).astype(bf16)
            matrix_ref[pl.ds(at + chan, chan), :] = (cos_table * a1 + sin_table * a0).astype(bf16)
        return carry

    lax.fori_loop(0, beams // 8, fill, 0)

    place = lax.broadcasted_iota(jnp.int32, (stations, n * local), 0)
    one_hot = jnp.where(place == station_ref[...], 1.0, 0.0).astype(bf16)
    lane_index = lax.broadcasted_iota(jnp.int32, taps_ref.shape, 1)
    own_taps = jnp.sum(jnp.where(lane_index == me, taps_ref[...], 0.0), axis=1, keepdims=True)
    own_taps = own_taps * (1.0 / math.sqrt(ANTENNAS_PER_STN * n))
    frame = lax.broadcasted_iota(jnp.int32, (stations2, 128), 1)

    def forward(h, lane, slot, target):
        return pltpu.make_async_remote_copy(
            src_ref=lanes_ref.at[h, lane], dst_ref=lanes_ref.at[h, lane],
            send_sem=g_send.at[slot], recv_sem=g_recv.at[h, lane],
            device_id=target, device_id_type=MESH,
        )

    def lane_of(r, c, s):
        return (r * n_col + c) * n_sub + s

    other_col = {"row": row, "col": 1 - col, "sub": sub}
    other_sub = {"row": row, "col": col, "sub": 1 - sub}
    sends = []

    def send(h, lane, target):
        copy = forward(h, lane, len(sends), target)
        copy.start()
        sends.append(copy)

    def arrived(h, lane):
        forward(h, lane, 0, other_sub).wait_recv()

    def filter_half(h, last):
        def finish_slab(step, carry):
            slab(h, step).wait_recv()
            return carry

        lax.fori_loop(1, n, finish_slab, 0)
        summed = jnp.concatenate(
            [
                jnp.dot(
                    one_hot, recv[h, q].reshape(n * local, width), preferred_element_type=f32
                )
                for q in range(2)
            ],
            axis=0,
        )
        for start in range(0, width, 128):
            tile = summed[:, start : start + 128]
            result = own_taps[0:1] * tile
            for tap in range(1, taps_ref.shape[0]):
                moved = jnp.where(
                    frame >= tap, pltpu.roll(tile, tap, 1), pltpu.roll(last, tap, 1)
                )
                result = result + own_taps[tap : tap + 1] * moved
            lanes_ref[h, me, :, start : start + 128] = result.astype(bf16)
            last = tile
        return last

    def spread_own(h):
        for step in range(1, n_row):
            send(h, me, {"row": lax.rem(row + step, n_row), "col": col, "sub": sub})
        send(h, me, other_col)
        send(h, me, other_sub)

    def spread_row(h):
        for step in range(1, n_row):
            lane = lane_of(lax.rem(row + n_row - step, n_row), col, sub)
            arrived(h, lane)
            send(h, lane, other_col)
            send(h, lane, other_sub)

    def spread_col(h):
        for step in range(n_row):
            lane = lane_of(lax.rem(row + n_row - step, n_row), 1 - col, sub)
            arrived(h, lane)
            send(h, lane, other_sub)

    last = jnp.zeros((stations2, 128), f32)
    for h in range(halves):
        last = filter_half(h, last)
        spread_own(h)
        if h > 0:
            spread_col(h - 1)
        spread_row(h)
    spread_col(halves - 1)
    for h in range(halves):
        for step in range(n_row):
            for c in range(n_col):
                arrived(h, lane_of(lax.rem(row + n_row - step, n_row), c, 1 - sub))
    for copy in sends:
        copy.wait_send()
    for h in range(halves):

        def finish_send(step, carry, h=h):
            slab(h, step).wait_send()
            return carry

        lax.fori_loop(1, n, finish_send, 0)
    for step in range(1, n_row):
        weight(step).wait_send()


def exchange(samples, w, station, taps, sgroup, bgroup, n_row, n_col, n_sub, halves):
    n = n_row * n_col * n_sub
    local, _, chan, frames = samples.shape
    stations = sgroup.shape[1]
    stations2 = 2 * stations
    width = frames // halves
    kqs, block = w.shape
    beams = block // n_row
    any_space = pl.BlockSpec(memory_space=pl.ANY)
    vmem = pl.BlockSpec(memory_space=pltpu.VMEM)
    dma = pltpu.SemaphoreType.DMA
    sends = ((n_row - 1) * 3 + 2 + n_row) * halves
    bf16 = jnp.bfloat16
    inputs = (samples, w, station, taps, sgroup, bgroup)
    return pl.pallas_call(
        functools.partial(exchange_kernel, n_row, n_col, n_sub),
        out_shape=(
            jax.ShapeDtypeStruct((halves, n, stations2, width), bf16),
            jax.ShapeDtypeStruct((beams * 2 * chan, chan * stations2), bf16),
        ),
        in_specs=[any_space] * 6,
        out_specs=(vmem, vmem),
        scratch_shapes=[pltpu.VMEM(a.shape, a.dtype) for a in inputs]
        + [
            pltpu.VMEM((chan, halves, 2, local, width), bf16),
            pltpu.VMEM((halves, 2, n, local, width), bf16),
            pltpu.VMEM((n_row, beams, kqs), bf16),
            pltpu.VMEM((n_row, beams, kqs), bf16),
            pltpu.VMEM((beams, chan * stations2), jnp.float32),
            pltpu.VMEM((beams, chan * stations2), jnp.float32),
            dma((len(inputs),)), dma((2,)), dma((halves, n)), dma((halves, n)),
            dma((n_row,)), dma((n_row,)), dma((sends,)), dma((halves, n)),
        ],
        compiler_params=pltpu.CompilerParams(
            collective_id=0, has_side_effects=True, vmem_limit_bytes=24 * 1024 * 1024
        ),
        name="exchange",
    )(*inputs)


def fourier(points):
    count = len(points)
    if count == 1:
        return points
    even, odd = fourier(points[0::2]), fourier(points[1::2])
    half = count // 2
    low, high = [], []
    for index in range(half):
        (er, ei), (r, i) = even[index], odd[index]
        if index == 0:
            tr, ti = r, i
        elif 4 * index == count:
            tr, ti = i, -r
        else:
            c, s = math.cos(2 * math.pi * index / count), math.sin(2 * math.pi * index / count)
            if 8 * index == count:
                tr, ti = (r + i) * c, (i - r) * c
            elif 8 * index == 3 * count:
                tr, ti = (i - r) * s, -(r + i) * s
            else:
                tr, ti = r * c + i * s, i * c - r * s
        low.append((er + tr, ei + ti))
        high.append((er - tr, ei - ti))
    return low + high

def beam_kernel(
    lanes_ref, matrix_ref, taps_ref, vis_ref, out_ref,
    spectra, gram, even_ref, odd_ref, wide_taps,
):
    halves, chan, stations2, width = lanes_ref.shape
    stations = stations2 // 2
    frames = halves * width
    step_index = pl.program_id(0)
    rows = out_ref.shape[0] // 2
    size = rows * 2 * chan
    count = matrix_ref.shape[0] // size

    def product(index):
        at = pl.multiple_of(index * size, size)
        return jnp.dot(
            matrix_ref[pl.ds(at, size), :],
            spectra[...].reshape(chan * stations2, frames),
            preferred_element_type=jnp.float32,
        )

    @pl.when(step_index == 0)
    def _():
        step_rows = 16

        @pl.loop(0, stations // step_rows)
        def _(block):
            low = pl.multiple_of(block * step_rows, step_rows)
            for start in range(0, frames, 128):
                h, inner = divmod(start, width)
                points = [
                    tuple(
                        lanes_ref[
                            h, c, pl.ds(low + q * stations, step_rows), inner : inner + 128
                        ].astype(jnp.float32)
                        for q in range(2)
                    )
                    for c in range(chan)
                ]
                for k, parts in enumerate(fourier(points)):
                    for q, value in enumerate(parts):
                        spectra[
                            k, pl.ds(low + q * stations, step_rows), start : start + 128
                        ] = value.astype(jnp.bfloat16)

        chan_rows, _, own, _ = vis_ref.shape
        first = lax.axis_index("row") * chan_rows
        block_index = lax.axis_index(("col", "sub"))
        begin = pl.multiple_of(block_index * own, own)
        for k in range(chan_rows):
            block = spectra[first + k]
            gram[k] = lax.dot_general(
                block, block, (((1,), (1,)), ((), ())), preferred_element_type=jnp.float32
            )
            top = gram[k, pl.ds(begin, own), :]
            bottom = gram[k, pl.ds(begin + stations, own), :]
            vis_ref[k, 0] = (top[:, :stations] + bottom[:, stations:]) * (1.0 / frames)
            vis_ref[k, 1] = (bottom[:, :stations] - top[:, stations:]) * (1.0 / frames)

        for tap in range(taps_ref.shape[0]):
            there = lax.broadcasted_iota(jnp.int32, (chan, chan), 1)
            here = lax.broadcasted_iota(jnp.int32, (chan, chan), 0)
            values = jnp.where(there == here, taps_ref[tap : tap + 1, :], 0.0)
            wide_taps[tap] = jnp.broadcast_to(
                jnp.sum(values, axis=1, keepdims=True), (chan, 128)
            )
        even_ref[...] = product(0)

    lane = lax.broadcasted_iota(jnp.int32, (chan, 128), 1)

    def shift(tiles, amount):
        turned = [pltpu.roll(tile, amount, 1) for tile in tiles]
        before = [jnp.zeros_like(turned[0])] + turned[:-1]
        return [jnp.where(lane >= amount, t, b) for t, b in zip(turned, before)]

    taps = taps_ref.shape[0]
    stride = 4

    def synthesize(inverse, offset):
        for index in range(2 * rows):
            tiles = [
                inverse[index * chan : (index + 1) * chan, start : start + 128]
                for start in range(0, frames, 128)
            ]
            moved = [tiles]
            for amount in range(1, stride):
                moved.append(shift(tiles, amount))
            total_tiles = None
            for high in range(taps // stride - 1, -1, -1):
                if total_tiles is not None:
                    total_tiles = shift(total_tiles, stride)
                for low in range(stride):
                    tap = wide_taps[high * stride + low]
                    terms = [tap * tile for tile in moved[low]]
                    total_tiles = (
                        terms
                        if total_tiles is None
                        else [a + t for a, t in zip(total_tiles, terms)]
                    )
            for number, tile in enumerate(total_tiles):
                out_ref[offset + index // 2, index % 2, :, number * 128 : (number + 1) * 128] = tile

    odd_ref[...] = product(2 * step_index + 1)
    synthesize(even_ref, 0)
    even_ref[...] = product(jnp.minimum(2 * step_index + 2, count - 1))
    synthesize(odd_ref, rows)


def beamform(lanes, matrix, taps, vis_shape, rows):
    halves, chan, stations2, width = lanes.shape
    frames = halves * width
    beams = matrix.shape[0] // (2 * chan)
    whole = lambda *shape: pl.BlockSpec(shape, lambda i: (0,) * len(shape))
    vmem = pl.BlockSpec(memory_space=pltpu.VMEM)
    return pl.pallas_call(
        beam_kernel,
        grid=(beams // (2 * rows),),
        out_shape=(
            jax.ShapeDtypeStruct(vis_shape, jnp.float32),
            jax.ShapeDtypeStruct((beams, 2, chan, frames), jnp.float32),
        ),
        in_specs=[vmem, vmem, vmem],
        out_specs=(
            whole(*vis_shape),
            pl.BlockSpec((2 * rows, 2, chan, frames), lambda i: (i, 0, 0, 0)),
        ),
        scratch_shapes=[
            pltpu.VMEM((chan, stations2, frames), jnp.bfloat16),
            pltpu.VMEM((vis_shape[0], stations2, stations2), jnp.float32),
            pltpu.VMEM((rows * 2 * chan, frames), jnp.float32),
            pltpu.VMEM((rows * 2 * chan, frames), jnp.float32),
            pltpu.VMEM((taps.shape[0], chan, 128), jnp.float32),
        ],
        compiler_params=pltpu.CompilerParams(
            dimension_semantics=("arbitrary",), vmem_limit_bytes=24 * 1024 * 1024
        ),
        name="beamform",
    )(lanes, matrix, taps)


def lane_body(
    samples, analysis_taps, synthesis_taps, antenna_station, station_group, beam_group, beam_weights
):
    n_row, n_col, n_sub = (lax.axis_size(name) for name in ("row", "col", "sub"))
    stations = station_group.shape[0]
    chan_rows, _, block, _ = beam_weights.shape
    w = beam_weights.transpose(0, 1, 3, 2).reshape(chan_rows * 2 * stations, block)
    lanes, matrix = exchange(
        samples, w, antenna_station.reshape(1, -1), analysis_taps,
        station_group.reshape(1, -1), beam_group.reshape(-1, 128), n_row, n_col, n_sub, 2,
    )
    tile_rows = stations // (n_col * n_sub)
    return beamform(lanes, matrix, synthesis_taps, (chan_rows, 2, tile_rows, stations), 8)


def solution(mesh):
    shape = mesh.shape
    fits = (
        shape["row"] * shape["col"] * shape["sub"] == 16 and shape["col"] == 2 and shape["sub"] == 2
    )
    return jax.shard_map(
        lane_body if fits else body,
        mesh=mesh,
        in_specs=(
            P(("grp", "row", "col", "sub"), None, None, None),
            P(),
            P(),
            P("grp"),
            P("grp", None),
            P("grp"),
            P(("grp", "row"), None, ("col", "sub"), None),
        ),
        out_specs=(
            P("row", None, ("grp", "col", "sub"), None),
            P(("grp", "col", "sub", "row"), None, None, None),
        ),
        check_vma=False,
    )
```

```python
import functools
import math

import jax
import jax.numpy as jnp
from jax import lax
from jax.experimental import pallas as pl
from jax.experimental.pallas import tpu as pltpu
from jax.sharding import PartitionSpec as P

MESH = pl.DeviceIdType.MESH

ANTENNAS_PER_STN = 8
SPEC = 512


def polyphase(signal, coefficients):
    length = signal.shape[-1]
    output = coefficients[0][:, None] * signal
    for tap_index in range(1, coefficients.shape[0]):
        shifted = jnp.pad(
            signal[..., : length - tap_index], [(0, 0)] * (signal.ndim - 1) + [(tap_index, 0)]
        )
        output = output + coefficients[tap_index][:, None] * shifted
    return output


def fourier_table(length, direction):
    indices = jnp.arange(length)
    angles = (
        2.0 * math.pi / length * (indices[:, None] * indices[None, :] % length).astype(jnp.float32)
    )
    cosine_part = jnp.cos(angles)
    sine_part = jnp.sin(angles)
    table = jnp.stack(
        [
            jnp.stack([cosine_part, direction * sine_part]),
            jnp.stack([-direction * sine_part, cosine_part]),
        ]
    )
    return table.transpose(0, 2, 1, 3) * (1.0 / math.sqrt(length))


def body(
    samples, analysis_taps, synthesis_taps, antenna_station, station_group, beam_group, beam_weights
):
    high = lax.Precision.HIGHEST
    block_count = lax.axis_size(("col", "sub"))
    block_index = lax.axis_index(("col", "sub"))
    filtered = polyphase(samples.astype(jnp.float32), analysis_taps)
    spectra = jnp.einsum(
        "aqcf,qcpk->apkf", filtered, fourier_table(samples.shape[2], -1.0), precision=high
    ).astype(jnp.bfloat16)
    turned = lax.all_to_all(spectra, "row", split_axis=2, concat_axis=0, tiled=True)
    local_count = spectra.shape[0]
    held_rows = turned.shape[0]
    chan_rows = turned.shape[2]
    spec_len = turned.shape[3]
    station_count = station_group.shape[0]
    flat_width = 2 * chan_rows * spec_len
    tile_rows = station_count // block_count
    shard_rows = lax.all_gather(turned, ("col", "sub"), axis=0, tiled=True)
    row_total = shard_rows.shape[0]
    positions = jnp.arange(row_total, dtype=jnp.int32)
    source_block = positions // held_rows
    offset_rows = positions % held_rows
    source_row = offset_rows // local_count
    antenna = offset_rows % local_count
    global_index = (source_row * block_count + source_block) * local_count + antenna
    targets = antenna_station[global_index]
    wanted = jnp.arange(station_count, dtype=jnp.int32)
    one_hot = (targets[None, :] == wanted[:, None]).astype(jnp.bfloat16)
    summed_values = jnp.dot(
        one_hot, shard_rows.reshape(row_total, flat_width), preferred_element_type=jnp.float32
    )
    flat_stations = (summed_values * (1.0 / math.sqrt(ANTENNAS_PER_STN))).astype(jnp.bfloat16)
    station_list = flat_stations.reshape(station_count, 2, chan_rows, spec_len)
    real_part = station_list[:, 0]
    imag_part = station_list[:, 1]
    own_rows = lax.dynamic_slice_in_dim(station_list, block_index * tile_rows, tile_rows, 0)
    own_real = own_rows[:, 0]
    own_imag = own_rows[:, 1]
    vis_real = (
        jnp.einsum("icf,jcf->cij", own_real, real_part, preferred_element_type=jnp.float32)
        + jnp.einsum("icf,jcf->cij", own_imag, imag_part, preferred_element_type=jnp.float32)
    ) * (1.0 / SPEC)
    vis_imag = (
        jnp.einsum("icf,jcf->cij", own_imag, real_part, preferred_element_type=jnp.float32)
        - jnp.einsum("icf,jcf->cij", own_real, imag_part, preferred_element_type=jnp.float32)
    ) * (1.0 / SPEC)
    visibilities = jnp.stack([vis_real, vis_imag], axis=1)
    beam_block = beam_weights.shape[2]
    own_groups = lax.dynamic_slice_in_dim(beam_group, block_index * beam_block, beam_block, 0)
    members = station_group[:, 0][None, :] == own_groups[:, None]
    scaling = 1.0 / jnp.sqrt(jnp.sum(members.astype(jnp.float32), axis=1))
    weights = jnp.where(members[None, None], beam_weights, jnp.zeros((), jnp.bfloat16))
    weight_real = weights[:, 0]
    imaginary_weight = weights[:, 1]
    beam_real = jnp.einsum(
        "cbs,scf->bcf", weight_real, real_part, preferred_element_type=jnp.float32
    ) - jnp.einsum("cbs,scf->bcf", imaginary_weight, imag_part, preferred_element_type=jnp.float32)
    beam_imag = jnp.einsum(
        "cbs,scf->bcf", weight_real, imag_part, preferred_element_type=jnp.float32
    ) + jnp.einsum("cbs,scf->bcf", imaginary_weight, real_part, preferred_element_type=jnp.float32)
    beams = (jnp.stack([beam_real, beam_imag], axis=1) * scaling[:, None, None, None]).astype(
        jnp.bfloat16
    )
    returned = lax.all_to_all(beams, "row", split_axis=0, concat_axis=2, tiled=True)
    inverse = jnp.einsum(
        "bqkf,qkpc->bpcf",
        returned.astype(jnp.float32),
        fourier_table(returned.shape[2], 1.0),
        precision=high,
    )
    beam_series = polyphase(inverse, synthesis_taps)
    return (visibilities, beam_series)


def exchange_kernel(
    n_row, n_col, n_sub,
    samples_hbm, w_hbm, station_hbm, taps_hbm, sgroup_hbm, bgroup_hbm,
    lanes_ref, matrix_ref,
    samples_ref, w_ref, station_ref, taps_ref, sgroup_ref, bgroup_ref,
    x_ref, recv, w_mine, w_all, plain_ref, swapped_ref,
    load_sem, own_sem, send_sem, recv_sem, w_send, w_recv, g_send, g_recv,
):
    n = n_row * n_col * n_sub
    row, col, sub = lax.axis_index("row"), lax.axis_index("col"), lax.axis_index("sub")
    me = (row * n_col + col) * n_sub + sub
    halves, _, stations2, width = lanes_ref.shape
    stations = stations2 // 2
    local = samples_ref.shape[0]
    chan = n
    f32, bf16 = jnp.float32, jnp.bfloat16

    def coords(index):
        return {
            "row": lax.div(index, n_col * n_sub),
            "col": lax.rem(lax.div(index, n_sub), n_col),
            "sub": lax.rem(index, n_sub),
        }

    barrier = pltpu.get_barrier_semaphore()

    def greet(step, carry):
        pl.semaphore_signal(
            barrier, inc=1, device_id=coords(lax.rem(me + step, n)), device_id_type=MESH
        )
        return carry

    lax.fori_loop(1, n, greet, 0)
    pairs = [
        (samples_hbm, samples_ref), (w_hbm, w_ref), (station_hbm, station_ref),
        (taps_hbm, taps_ref), (sgroup_hbm, sgroup_ref), (bgroup_hbm, bgroup_ref),
    ]
    loads = [pltpu.make_async_copy(a, b, load_sem.at[i]) for i, (a, b) in enumerate(pairs)]
    for load in loads:
        load.start()

    total = local * 2 * chan
    block = 128
    loads[0].wait()
    source = samples_ref[...].reshape(total, halves * width)
    for start in range(0, total, block):
        to = lax.broadcasted_iota(jnp.int32, (block, total), 0) + start
        origin = lax.broadcasted_iota(jnp.int32, (block, total), 1)
        wanted = (
            lax.rem(to, local) * (2 * chan)
            + lax.rem(lax.div(to, local), 2) * chan
            + lax.div(to, 2 * local)
        )
        turn = jnp.where(origin == wanted, 1.0, 0.0).astype(bf16)
        turned = jnp.dot(turn, source, preferred_element_type=f32).astype(bf16)
        lanes_here = block // (2 * local)
        first = start // (2 * local)
        for h in range(halves):
            x_ref[first : first + lanes_here, h] = turned[:, h * width : (h + 1) * width].reshape(
                lanes_here, 2, local, width
            )
    for load in loads[1:]:
        load.wait()
    beams = w_mine.shape[1]
    flipped = w_ref[...].astype(f32).T.astype(bf16)
    for r in range(n_row):
        w_mine[r] = flipped[r * beams : (r + 1) * beams]
    for h in range(halves):
        recv[h, :, me] = x_ref[me, h]
    w_all[row] = w_mine[row]

    pl.semaphore_wait(barrier, n - 1)

    def slab(h, step):
        peer = lax.rem(me + step, n)
        return pltpu.make_async_remote_copy(
            src_ref=x_ref.at[peer, h], dst_ref=recv.at[h, :, me],
            send_sem=send_sem.at[h, step], recv_sem=recv_sem.at[h, step],
            device_id=coords(peer), device_id_type=MESH,
        )

    def weight(step):
        peer = lax.rem(row + step, n_row)
        return pltpu.make_async_remote_copy(
            src_ref=w_mine.at[peer], dst_ref=w_all.at[row],
            send_sem=w_send.at[step], recv_sem=w_recv.at[step],
            device_id={"row": peer, "col": col, "sub": sub}, device_id_type=MESH,
        )

    for step in range(1, n_row):
        weight(step).start()
    for h in range(halves):

        def start_slab(step, carry, h=h):
            slab(h, step).start()
            return carry

        lax.fori_loop(1, n, start_slab, 0)

    def column(values, offset, size):
        there = lax.broadcasted_iota(jnp.int32, (size, values.shape[1]), 1)
        here = lax.broadcasted_iota(jnp.int32, (size, values.shape[1]), 0) + offset
        return jnp.sum(jnp.where(there == here, values, 0.0), axis=1, keepdims=True)

    across = bgroup_ref.shape[1]
    begin = ((col * n_sub + sub) * n_row + row) * beams
    own_groups = column(
        bgroup_ref[pl.ds(lax.div(begin, across), 1), :].astype(f32), lax.rem(begin, across), beams
    )
    groups = sgroup_ref[...].astype(f32)
    members = jnp.where(groups == own_groups, 1.0, 0.0)
    scaling = 1.0 / jnp.sqrt(jnp.sum(members, axis=1, keepdims=True))
    mask = jnp.concatenate([members] * (128 // stations), axis=1)
    mask = jnp.concatenate([mask] * (chan * stations2 // 128), axis=1)
    for step in range(1, n_row):
        weight(step).wait_recv()
    columns = chan * stations2
    weights = jnp.concatenate([w_all[r] for r in range(n_row)], axis=1).astype(f32)
    weights = jnp.where(mask > 0.5, weights, 0.0) * scaling
    position = lax.broadcasted_iota(jnp.int32, (beams, columns), 1)
    first_half = lax.rem(position, stations2) < stations
    plain_ref[...] = jnp.where(first_half, weights, -weights)
    swapped_ref[...] = jnp.where(
        first_half, pltpu.roll(weights, columns - stations, 1), pltpu.roll(weights, stations, 1)
    )
    turn_index = lax.rem(
        lax.broadcasted_iota(jnp.int32, (chan, columns), 0)
        * lax.div(lax.broadcasted_iota(jnp.int32, (chan, columns), 1), stations2),
        chan,
    )
    cos_table = jnp.zeros((chan, columns), f32)
    sin_table = jnp.zeros((chan, columns), f32)
    for m in range(chan):
        angle = 2 * math.pi * m / chan
        hit = turn_index == m
        cos_table = jnp.where(hit, math.cos(angle) / math.sqrt(chan), cos_table)
        sin_table = jnp.where(hit, math.sin(angle) / math.sqrt(chan), sin_table)

    def fill(index, carry):
        low = pl.multiple_of(index * 8, 8)
        plain, swapped = plain_ref[pl.ds(low, 8), :], swapped_ref[pl.ds(low, 8), :]
        for b in range(8):
            a0, a1 = plain[b : b + 1], swapped[b : b + 1]
            at = pl.multiple_of((low + b) * 2 * chan, 2 * chan)
            matrix_ref[pl.ds(at, chan), :] = (cos_table * a0 - sin_table * a1).astype(bf16)
            matrix_ref[pl.ds(at + chan, chan), :] = (cos_table * a1 + sin_table * a0).astype(bf16)
        return carry

    lax.fori_loop(0, beams // 8, fill, 0)

    place = lax.broadcasted_iota(jnp.int32, (stations, n * local), 0)
    one_hot = jnp.where(place == station_ref[...], 1.0, 0.0).astype(bf16)
    lane_index = lax.broadcasted_iota(jnp.int32, taps_ref.shape, 1)
    own_taps = jnp.sum(jnp.where(lane_index == me, taps_ref[...], 0.0), axis=1, keepdims=True)
    own_taps = own_taps * (1.0 / math.sqrt(ANTENNAS_PER_STN * n))
    frame = lax.broadcasted_iota(jnp.int32, (stations2, 128), 1)

    def forward(h, lane, slot, target):
        return pltpu.make_async_remote_copy(
            src_ref=lanes_ref.at[h, lane], dst_ref=lanes_ref.at[h, lane],
            send_sem=g_send.at[slot], recv_sem=g_recv.at[h, lane],
            device_id=target, device_id_type=MESH,
        )

    def lane_of(r, c, s):
        return (r * n_col + c) * n_sub + s

    other_col = {"row": row, "col": 1 - col, "sub": sub}
    other_sub = {"row": row, "col": col, "sub": 1 - sub}
    sends = []

    def send(h, lane, target):
        copy = forward(h, lane, len(sends), target)
        copy.start()
        sends.append(copy)

    def arrived(h, lane):
        forward(h, lane, 0, other_sub).wait_recv()

    def filter_half(h, last):
        def finish_slab(step, carry):
            slab(h, step).wait_recv()
            return carry

        lax.fori_loop(1, n, finish_slab, 0)
        summed = jnp.concatenate(
            [
                jnp.dot(
                    one_hot, recv[h, q].reshape(n * local, width), preferred_element_type=f32
                )
                for q in range(2)
            ],
            axis=0,
        )
        for start in range(0, width, 128):
            tile = summed[:, start : start + 128]
            result = own_taps[0:1] * tile
            for tap in range(1, taps_ref.shape[0]):
                moved = jnp.where(
                    frame >= tap, pltpu.roll(tile, tap, 1), pltpu.roll(last, tap, 1)
                )
                result = result + own_taps[tap : tap + 1] * moved
            lanes_ref[h, me, :, start : start + 128] = result.astype(bf16)
            last = tile
        return last

    def spread_own(h):
        for step in range(1, n_row):
            send(h, me, {"row": lax.rem(row + step, n_row), "col": col, "sub": sub})
        send(h, me, other_col)
        send(h, me, other_sub)

    def spread_row(h):
        for step in range(1, n_row):
            lane = lane_of(lax.rem(row + n_row - step, n_row), col, sub)
            arrived(h, lane)
            send(h, lane, other_col)
            send(h, lane, other_sub)

    def spread_col(h):
        for step in range(n_row):
            lane = lane_of(lax.rem(row + n_row - step, n_row), 1 - col, sub)
            arrived(h, lane)
            send(h, lane, other_sub)

    last = jnp.zeros((stations2, 128), f32)
    for h in range(halves):
        last = filter_half(h, last)
        spread_own(h)
        if h > 0:
            spread_col(h - 1)
        spread_row(h)
    spread_col(halves - 1)
    for h in range(halves):
        for step in range(n_row):
            for c in range(n_col):
                arrived(h, lane_of(lax.rem(row + n_row - step, n_row), c, 1 - sub))
    for copy in sends:
        copy.wait_send()
    for h in range(halves):

        def finish_send(step, carry, h=h):
            slab(h, step).wait_send()
            return carry

        lax.fori_loop(1, n, finish_send, 0)
    for step in range(1, n_row):
        weight(step).wait_send()


def exchange(samples, w, station, taps, sgroup, bgroup, n_row, n_col, n_sub, halves):
    n = n_row * n_col * n_sub
    local, _, chan, frames = samples.shape
    stations = sgroup.shape[1]
    stations2 = 2 * stations
    width = frames // halves
    kqs, block = w.shape
    beams = block // n_row
    any_space = pl.BlockSpec(memory_space=pltpu.HBM)
    vmem = pl.BlockSpec(memory_space=pltpu.VMEM)
    dma = pltpu.SemaphoreType.DMA
    sends = ((n_row - 1) * 3 + 2 + n_row) * halves
    bf16 = jnp.bfloat16
    inputs = (samples, w, station, taps, sgroup, bgroup)
    return pl.pallas_call(
        functools.partial(exchange_kernel, n_row, n_col, n_sub),
        out_shape=(
            jax.ShapeDtypeStruct((halves, n, stations2, width), bf16),
            jax.ShapeDtypeStruct((beams * 2 * chan, chan * stations2), bf16),
        ),
        in_specs=[any_space] * 6,
        out_specs=(vmem, vmem),
        scratch_shapes=[pltpu.VMEM(a.shape, a.dtype) for a in inputs]
        + [
            pltpu.VMEM((chan, halves, 2, local, width), bf16),
            pltpu.VMEM((halves, 2, n, local, width), bf16),
            pltpu.VMEM((n_row, beams, kqs), bf16),
            pltpu.VMEM((n_row, beams, kqs), bf16),
            pltpu.VMEM((beams, chan * stations2), jnp.float32),
            pltpu.VMEM((beams, chan * stations2), jnp.float32),
            dma((len(inputs),)), dma((2,)), dma((halves, n)), dma((halves, n)),
            dma((n_row,)), dma((n_row,)), dma((sends,)), dma((halves, n)),
        ],
        compiler_params=pltpu.CompilerParams(
            collective_id=0, has_side_effects=True, vmem_limit_bytes=24 * 1024 * 1024
        ),
        name="exchange",
    )(*inputs)


def fourier(points):
    count = len(points)
    if count == 1:
        return points
    even, odd = fourier(points[0::2]), fourier(points[1::2])
    half = count // 2
    low, high = [], []
    for index in range(half):
        (er, ei), (r, i) = even[index], odd[index]
        if index == 0:
            tr, ti = r, i
        elif 4 * index == count:
            tr, ti = i, -r
        else:
            c, s = math.cos(2 * math.pi * index / count), math.sin(2 * math.pi * index / count)
            if 8 * index == count:
                tr, ti = (r + i) * c, (i - r) * c
            elif 8 * index == 3 * count:
                tr, ti = (i - r) * s, -(r + i) * s
            else:
                tr, ti = r * c + i * s, i * c - r * s
        low.append((er + tr, ei + ti))
        high.append((er - tr, ei - ti))
    return low + high

def beam_kernel(
    lanes_ref, matrix_ref, taps_ref, vis_ref, out_ref,
    spectra, gram, inverse_ref, wide_taps,
):
    halves, chan, stations2, width = lanes_ref.shape
    stations = stations2 // 2
    frames = halves * width
    step_index = pl.program_id(0)
    size = out_ref.shape[0]

    def product(index):
        at = pl.multiple_of(index * size, size)
        return jnp.dot(
            matrix_ref[pl.ds(at, size), :],
            spectra[...].reshape(chan * stations2, frames),
            preferred_element_type=jnp.float32,
        )

    @pl.when(step_index == 0)
    def _():
        step_rows = 16

        @pl.loop(0, stations // step_rows)
        def _(block):
            low = pl.multiple_of(block * step_rows, step_rows)
            for start in range(0, frames, 128):
                h, inner = divmod(start, width)
                points = [
                    tuple(
                        lanes_ref[
                            h, c, pl.ds(low + q * stations, step_rows), inner : inner + 128
                        ].astype(jnp.float32)
                        for q in range(2)
                    )
                    for c in range(chan)
                ]
                for k, parts in enumerate(fourier(points)):
                    for q, value in enumerate(parts):
                        spectra[
                            k, pl.ds(low + q * stations, step_rows), start : start + 128
                        ] = value.astype(jnp.bfloat16)

        chan_rows, _, own, _ = vis_ref.shape
        first = lax.axis_index("row") * chan_rows
        block_index = lax.axis_index(("col", "sub"))
        begin = pl.multiple_of(block_index * own, own)
        for k in range(chan_rows):
            block = spectra[first + k]
            gram[k] = lax.dot_general(
                block, block, (((1,), (1,)), ((), ())), preferred_element_type=jnp.float32
            )
            top = gram[k, pl.ds(begin, own), :]
            bottom = gram[k, pl.ds(begin + stations, own), :]
            vis_ref[k, 0] = (top[:, :stations] + bottom[:, stations:]) * (1.0 / frames)
            vis_ref[k, 1] = (bottom[:, :stations] - top[:, stations:]) * (1.0 / frames)

        for tap in range(taps_ref.shape[0]):
            there = lax.broadcasted_iota(jnp.int32, (chan, chan), 1)
            here = lax.broadcasted_iota(jnp.int32, (chan, chan), 0)
            values = jnp.where(there == here, taps_ref[tap : tap + 1, :], 0.0)
            wide_taps[tap] = jnp.broadcast_to(
                jnp.sum(values, axis=1, keepdims=True), (chan, 128)
            )

    lane = lax.broadcasted_iota(jnp.int32, (8, 128), 1)
    later = [None] + [lane >= amount for amount in range(1, taps_ref.shape[0])]

    def shift(tiles, amount):
        turned = [pltpu.roll(tile, amount, 1) for tile in tiles]
        before = [jnp.zeros_like(turned[0])] + turned[:-1]
        return [jnp.where(later[amount], t, b) for t, b in zip(turned, before)]

    taps = taps_ref.shape[0]
    stride = 4
    starts = range(0, frames, 128)

    inverse_ref[...] = product(step_index)
    for top in range(0, chan, 8):
        tap_tiles = [wide_taps[tap, top : top + 8, :] for tap in range(taps)]

        def one(index, carry, top=top, tap_tiles=tap_tiles):
            at = pl.multiple_of(index * chan + top, 8)
            tiles = [inverse_ref[pl.ds(at, 8), start : start + 128] for start in starts]
            moved = [tiles] + [shift(tiles, amount) for amount in range(1, stride)]
            total_tiles = None
            for high in range(taps // stride - 1, -1, -1):
                if total_tiles is not None:
                    total_tiles = shift(total_tiles, stride)
                for low in range(stride):
                    tap = tap_tiles[high * stride + low]
                    terms = [tap * tile for tile in moved[low]]
                    total_tiles = (
                        terms
                        if total_tiles is None
                        else [a + t for a, t in zip(total_tiles, terms)]
                    )
            for start, tile in zip(starts, total_tiles):
                out_ref[pl.ds(at, 8), start : start + 128] = tile
            return carry

        lax.fori_loop(0, size // chan, one, 0, unroll=16)


def beamform(lanes, matrix, taps, vis_shape, rows):
    halves, chan, stations2, width = lanes.shape
    frames = halves * width
    beams = matrix.shape[0] // (2 * chan)
    whole = lambda *shape: pl.BlockSpec(shape, lambda i: (0,) * len(shape))
    vmem = pl.BlockSpec(memory_space=pltpu.VMEM)
    vis, series = pl.pallas_call(
        beam_kernel,
        grid=(beams // rows,),
        out_shape=(
            jax.ShapeDtypeStruct(vis_shape, jnp.float32),
            jax.ShapeDtypeStruct((matrix.shape[0], frames), jnp.float32),
        ),
        in_specs=[vmem, vmem, vmem],
        out_specs=(
            whole(*vis_shape),
            pl.BlockSpec((rows * 2 * chan, frames), lambda i: (i, 0)),
        ),
        scratch_shapes=[
            pltpu.VMEM((chan, stations2, frames), jnp.bfloat16),
            pltpu.VMEM((vis_shape[0], stations2, stations2), jnp.float32),
            pltpu.VMEM((rows * 2 * chan, frames), jnp.float32),
            pltpu.VMEM((taps.shape[0], chan, 128), jnp.float32),
        ],
        compiler_params=pltpu.CompilerParams(
            dimension_semantics=("arbitrary",), vmem_limit_bytes=24 * 1024 * 1024
        ),
        name="beamform",
    )(lanes, matrix, taps)
    return vis, series.reshape(beams, 2, chan, frames)


def lane_body(
    samples, analysis_taps, synthesis_taps, antenna_station, station_group, beam_group, beam_weights
):
    n_row, n_col, n_sub = (lax.axis_size(name) for name in ("row", "col", "sub"))
    stations = station_group.shape[0]
    chan_rows, _, block, _ = beam_weights.shape
    w = beam_weights.transpose(0, 1, 3, 2).reshape(chan_rows * 2 * stations, block)
    lanes, matrix = exchange(
        samples, w, antenna_station.reshape(1, -1), analysis_taps,
        station_group.reshape(1, -1), beam_group.reshape(-1, 128), n_row, n_col, n_sub, 2,
    )
    tile_rows = stations // (n_col * n_sub)
    return beamform(lanes, matrix, synthesis_taps, (chan_rows, 2, tile_rows, stations), 8)


def solution(mesh):
    shape = mesh.shape
    fits = (
        shape["row"] * shape["col"] * shape["sub"] == 16 and shape["col"] == 2 and shape["sub"] == 2
    )
    return jax.shard_map(
        lane_body if fits else body,
        mesh=mesh,
        in_specs=(
            P(("grp", "row", "col", "sub"), None, None, None),
            P(),
            P(),
            P("grp"),
            P("grp", None),
            P("grp"),
            P(("grp", "row"), None, ("col", "sub"), None),
        ),
        out_specs=(
            P("row", None, ("grp", "col", "sub"), None),
            P(("grp", "col", "sub", "row"), None, None, None),
        ),
        check_vma=False,
    )
```

```python
import functools
import math

import jax
import jax.numpy as jnp
from jax import lax
from jax.experimental import pallas as pl
from jax.experimental.pallas import tpu as pltpu
from jax.sharding import PartitionSpec as P

MESH = pl.DeviceIdType.MESH

ANTENNAS_PER_STN = 8
SPEC = 512


def polyphase(signal, coefficients):
    length = signal.shape[-1]
    output = coefficients[0][:, None] * signal
    for tap_index in range(1, coefficients.shape[0]):
        shifted = jnp.pad(
            signal[..., : length - tap_index], [(0, 0)] * (signal.ndim - 1) + [(tap_index, 0)]
        )
        output = output + coefficients[tap_index][:, None] * shifted
    return output


def fourier_table(length, direction):
    indices = jnp.arange(length)
    angles = (
        2.0 * math.pi / length * (indices[:, None] * indices[None, :] % length).astype(jnp.float32)
    )
    cosine_part = jnp.cos(angles)
    sine_part = jnp.sin(angles)
    table = jnp.stack(
        [
            jnp.stack([cosine_part, direction * sine_part]),
            jnp.stack([-direction * sine_part, cosine_part]),
        ]
    )
    return table.transpose(0, 2, 1, 3) * (1.0 / math.sqrt(length))


def body(
    samples, analysis_taps, synthesis_taps, antenna_station, station_group, beam_group, beam_weights
):
    high = lax.Precision.HIGHEST
    block_count = lax.axis_size(("col", "sub"))
    block_index = lax.axis_index(("col", "sub"))
    filtered = polyphase(samples.astype(jnp.float32), analysis_taps)
    spectra = jnp.einsum(
        "aqcf,qcpk->apkf", filtered, fourier_table(samples.shape[2], -1.0), precision=high
    ).astype(jnp.bfloat16)
    turned = lax.all_to_all(spectra, "row", split_axis=2, concat_axis=0, tiled=True)
    local_count = spectra.shape[0]
    held_rows = turned.shape[0]
    chan_rows = turned.shape[2]
    spec_len = turned.shape[3]
    station_count = station_group.shape[0]
    flat_width = 2 * chan_rows * spec_len
    tile_rows = station_count // block_count
    shard_rows = lax.all_gather(turned, ("col", "sub"), axis=0, tiled=True)
    row_total = shard_rows.shape[0]
    positions = jnp.arange(row_total, dtype=jnp.int32)
    source_block = positions // held_rows
    offset_rows = positions % held_rows
    source_row = offset_rows // local_count
    antenna = offset_rows % local_count
    global_index = (source_row * block_count + source_block) * local_count + antenna
    targets = antenna_station[global_index]
    wanted = jnp.arange(station_count, dtype=jnp.int32)
    one_hot = (targets[None, :] == wanted[:, None]).astype(jnp.bfloat16)
    summed_values = jnp.dot(
        one_hot, shard_rows.reshape(row_total, flat_width), preferred_element_type=jnp.float32
    )
    flat_stations = (summed_values * (1.0 / math.sqrt(ANTENNAS_PER_STN))).astype(jnp.bfloat16)
    station_list = flat_stations.reshape(station_count, 2, chan_rows, spec_len)
    real_part = station_list[:, 0]
    imag_part = station_list[:, 1]
    own_rows = lax.dynamic_slice_in_dim(station_list, block_index * tile_rows, tile_rows, 0)
    own_real = own_rows[:, 0]
    own_imag = own_rows[:, 1]
    vis_real = (
        jnp.einsum("icf,jcf->cij", own_real, real_part, preferred_element_type=jnp.float32)
        + jnp.einsum("icf,jcf->cij", own_imag, imag_part, preferred_element_type=jnp.float32)
    ) * (1.0 / SPEC)
    vis_imag = (
        jnp.einsum("icf,jcf->cij", own_imag, real_part, preferred_element_type=jnp.float32)
        - jnp.einsum("icf,jcf->cij", own_real, imag_part, preferred_element_type=jnp.float32)
    ) * (1.0 / SPEC)
    visibilities = jnp.stack([vis_real, vis_imag], axis=1)
    beam_block = beam_weights.shape[2]
    own_groups = lax.dynamic_slice_in_dim(beam_group, block_index * beam_block, beam_block, 0)
    members = station_group[:, 0][None, :] == own_groups[:, None]
    scaling = 1.0 / jnp.sqrt(jnp.sum(members.astype(jnp.float32), axis=1))
    weights = jnp.where(members[None, None], beam_weights, jnp.zeros((), jnp.bfloat16))
    weight_real = weights[:, 0]
    imaginary_weight = weights[:, 1]
    beam_real = jnp.einsum(
        "cbs,scf->bcf", weight_real, real_part, preferred_element_type=jnp.float32
    ) - jnp.einsum("cbs,scf->bcf", imaginary_weight, imag_part, preferred_element_type=jnp.float32)
    beam_imag = jnp.einsum(
        "cbs,scf->bcf", weight_real, imag_part, preferred_element_type=jnp.float32
    ) + jnp.einsum("cbs,scf->bcf", imaginary_weight, real_part, preferred_element_type=jnp.float32)
    beams = (jnp.stack([beam_real, beam_imag], axis=1) * scaling[:, None, None, None]).astype(
        jnp.bfloat16
    )
    returned = lax.all_to_all(beams, "row", split_axis=0, concat_axis=2, tiled=True)
    inverse = jnp.einsum(
        "bqkf,qkpc->bpcf",
        returned.astype(jnp.float32),
        fourier_table(returned.shape[2], 1.0),
        precision=high,
    )
    beam_series = polyphase(inverse, synthesis_taps)
    return (visibilities, beam_series)


def exchange_kernel(
    n_row, n_col, n_sub,
    samples_hbm, w_hbm, station_hbm, taps_hbm, sgroup_hbm, bgroup_hbm,
    lanes_ref, matrix_hbm,
    matrix_ref, samples_ref, w_ref, station_ref, taps_ref, sgroup_ref, bgroup_ref,
    x_ref, recv, w_mine, w_all, plain_ref, swapped_ref,
    load_sem, own_sem, send_sem, recv_sem, w_send, w_recv, g_send, g_recv,
):
    n = n_row * n_col * n_sub
    row, col, sub = lax.axis_index("row"), lax.axis_index("col"), lax.axis_index("sub")
    me = (row * n_col + col) * n_sub + sub
    halves, _, stations2, width = lanes_ref.shape
    stations = stations2 // 2
    local = samples_ref.shape[0]
    chan = n
    f32, bf16 = jnp.float32, jnp.bfloat16

    def coords(index):
        return {
            "row": lax.div(index, n_col * n_sub),
            "col": lax.rem(lax.div(index, n_sub), n_col),
            "sub": lax.rem(index, n_sub),
        }

    barrier = pltpu.get_barrier_semaphore()

    def greet(step, carry):
        pl.semaphore_signal(
            barrier, inc=1, device_id=coords(lax.rem(me + step, n)), device_id_type=MESH
        )
        return carry

    lax.fori_loop(1, n, greet, 0)
    pairs = [
        (samples_hbm, samples_ref), (w_hbm, w_ref), (station_hbm, station_ref),
        (taps_hbm, taps_ref), (sgroup_hbm, sgroup_ref), (bgroup_hbm, bgroup_ref),
    ]
    loads = [pltpu.make_async_copy(a, b, load_sem.at[i]) for i, (a, b) in enumerate(pairs)]
    for load in loads:
        load.start()

    total = local * 2 * chan
    block = 128
    loads[0].wait()
    source = samples_ref[...].reshape(total, halves * width)
    for start in range(0, total, block):
        to = lax.broadcasted_iota(jnp.int32, (block, total), 0) + start
        origin = lax.broadcasted_iota(jnp.int32, (block, total), 1)
        wanted = (
            lax.rem(to, local) * (2 * chan)
            + lax.rem(lax.div(to, local), 2) * chan
            + lax.div(to, 2 * local)
        )
        turn = jnp.where(origin == wanted, 1.0, 0.0).astype(bf16)
        turned = jnp.dot(turn, source, preferred_element_type=f32).astype(bf16)
        lanes_here = block // (2 * local)
        first = start // (2 * local)
        for h in range(halves):
            x_ref[first : first + lanes_here, h] = turned[:, h * width : (h + 1) * width].reshape(
                lanes_here, 2, local, width
            )
    for load in loads[1:]:
        load.wait()
    beams = w_mine.shape[1]
    flipped = w_ref[...].astype(f32).T.astype(bf16)
    for r in range(n_row):
        w_mine[r] = flipped[r * beams : (r + 1) * beams]
    for h in range(halves):
        recv[h, :, me] = x_ref[me, h]
    w_all[row] = w_mine[row]

    pl.semaphore_wait(barrier, n - 1)

    def slab(h, step):
        peer = lax.rem(me + step, n)
        return pltpu.make_async_remote_copy(
            src_ref=x_ref.at[peer, h], dst_ref=recv.at[h, :, me],
            send_sem=send_sem.at[h, step], recv_sem=recv_sem.at[h, step],
            device_id=coords(peer), device_id_type=MESH,
        )

    def weight(step):
        peer = lax.rem(row + step, n_row)
        return pltpu.make_async_remote_copy(
            src_ref=w_mine.at[peer], dst_ref=w_all.at[row],
            send_sem=w_send.at[step], recv_sem=w_recv.at[step],
            device_id={"row": peer, "col": col, "sub": sub}, device_id_type=MESH,
        )

    for step in range(1, n_row):
        weight(step).start()

    def start_half(h):
        def start_slab(step, carry):
            slab(h, step).start()
            return carry

        lax.fori_loop(1, n, start_slab, 0)

    def finish_half(h):
        def finish_send(step, carry):
            slab(h, step).wait_send()
            return carry

        lax.fori_loop(1, n, finish_send, 0)

    start_half(0)

    def column(values, offset, size):
        there = lax.broadcasted_iota(jnp.int32, (size, values.shape[1]), 1)
        here = lax.broadcasted_iota(jnp.int32, (size, values.shape[1]), 0) + offset
        return jnp.sum(jnp.where(there == here, values, 0.0), axis=1, keepdims=True)

    across = bgroup_ref.shape[1]
    begin = ((col * n_sub + sub) * n_row + row) * beams
    own_groups = column(
        bgroup_ref[pl.ds(lax.div(begin, across), 1), :].astype(f32), lax.rem(begin, across), beams
    )
    groups = sgroup_ref[...].astype(f32)
    members = jnp.where(groups == own_groups, 1.0, 0.0)
    scaling = 1.0 / jnp.sqrt(jnp.sum(members, axis=1, keepdims=True))
    mask = jnp.concatenate([members] * (128 // stations), axis=1)
    mask = jnp.concatenate([mask] * (chan * stations2 // 128), axis=1)
    for step in range(1, n_row):
        weight(step).wait_recv()
    columns = chan * stations2
    weights = jnp.concatenate([w_all[r] for r in range(n_row)], axis=1).astype(f32)
    weights = jnp.where(mask > 0.5, weights, 0.0) * scaling
    position = lax.broadcasted_iota(jnp.int32, (beams, columns), 1)
    first_half = lax.rem(position, stations2) < stations
    plain_ref[...] = jnp.where(first_half, weights, -weights)
    swapped_ref[...] = jnp.where(
        first_half, pltpu.roll(weights, columns - stations, 1), pltpu.roll(weights, stations, 1)
    )
    turn_index = lax.rem(
        lax.broadcasted_iota(jnp.int32, (chan, columns), 0)
        * lax.div(lax.broadcasted_iota(jnp.int32, (chan, columns), 1), stations2),
        chan,
    )
    cos_table = jnp.zeros((chan, columns), f32)
    sin_table = jnp.zeros((chan, columns), f32)
    for m in range(chan):
        angle = 2 * math.pi * m / chan
        hit = turn_index == m
        cos_table = jnp.where(hit, math.cos(angle) / math.sqrt(chan), cos_table)
        sin_table = jnp.where(hit, math.sin(angle) / math.sqrt(chan), sin_table)

    def fill(index, carry):
        low = pl.multiple_of(index * 8, 8)
        plain, swapped = plain_ref[pl.ds(low, 8), :], swapped_ref[pl.ds(low, 8), :]
        for b in range(8):
            a0, a1 = plain[b : b + 1], swapped[b : b + 1]
            at = pl.multiple_of((low + b) * 2 * chan, 2 * chan)
            matrix_ref[pl.ds(at, chan), :] = (cos_table * a0 - sin_table * a1).astype(bf16)
            matrix_ref[pl.ds(at + chan, chan), :] = (cos_table * a1 + sin_table * a0).astype(bf16)
        return carry

    lax.fori_loop(0, beams // 8, fill, 0)
    matrix_copy = pltpu.make_async_copy(matrix_ref, matrix_hbm, own_sem.at[0])
    matrix_copy.start()

    place = lax.broadcasted_iota(jnp.int32, (stations, n * local), 0)
    one_hot = jnp.where(place == station_ref[...], 1.0, 0.0).astype(bf16)
    lane_index = lax.broadcasted_iota(jnp.int32, taps_ref.shape, 1)
    own_taps = jnp.sum(jnp.where(lane_index == me, taps_ref[...], 0.0), axis=1, keepdims=True)
    own_taps = own_taps * (1.0 / math.sqrt(ANTENNAS_PER_STN * n))
    frame = lax.broadcasted_iota(jnp.int32, (stations2, 128), 1)

    def forward(h, lane, slot, target):
        return pltpu.make_async_remote_copy(
            src_ref=lanes_ref.at[h, lane], dst_ref=lanes_ref.at[h, lane],
            send_sem=g_send.at[slot], recv_sem=g_recv.at[h, lane],
            device_id=target, device_id_type=MESH,
        )

    def lane_of(r, c, s):
        return (r * n_col + c) * n_sub + s

    other_col = {"row": row, "col": 1 - col, "sub": sub}
    other_sub = {"row": row, "col": col, "sub": 1 - sub}
    sends = []

    def send(h, lane, target):
        copy = forward(h, lane, len(sends), target)
        copy.start()
        sends.append(copy)

    def arrived(h, lane):
        forward(h, lane, 0, other_sub).wait_recv()

    def filter_half(h, last):
        def finish_slab(step, carry):
            slab(h, step).wait_recv()
            return carry

        lax.fori_loop(1, n, finish_slab, 0)
        summed = jnp.concatenate(
            [
                jnp.dot(
                    one_hot, recv[h, q].reshape(n * local, width), preferred_element_type=f32
                )
                for q in range(2)
            ],
            axis=0,
        )
        for start in range(0, width, 128):
            tile = summed[:, start : start + 128]
            result = own_taps[0:1] * tile
            for tap in range(1, taps_ref.shape[0]):
                moved = jnp.where(
                    frame >= tap, pltpu.roll(tile, tap, 1), pltpu.roll(last, tap, 1)
                )
                result = result + own_taps[tap : tap + 1] * moved
            lanes_ref[h, me, :, start : start + 128] = result.astype(bf16)
            last = tile
        return last

    def spread_own(h):
        for step in range(1, n_row):
            send(h, me, {"row": lax.rem(row + step, n_row), "col": col, "sub": sub})
        send(h, me, other_col)
        send(h, me, other_sub)

    def spread_row(h):
        for step in range(1, n_row):
            lane = lane_of(lax.rem(row + n_row - step, n_row), col, sub)
            arrived(h, lane)
            send(h, lane, other_col)
            send(h, lane, other_sub)

    def spread_col(h):
        for step in range(n_row):
            lane = lane_of(lax.rem(row + n_row - step, n_row), 1 - col, sub)
            arrived(h, lane)
            send(h, lane, other_sub)

    last = jnp.zeros((stations2, 128), f32)
    for h in range(halves):
        if h + 1 < halves:
            finish_half(h)
            start_half(h + 1)
        last = filter_half(h, last)
        spread_own(h)
        if h > 0:
            spread_col(h - 1)
        spread_row(h)
    spread_col(halves - 1)
    for h in range(halves):
        for step in range(n_row):
            for c in range(n_col):
                arrived(h, lane_of(lax.rem(row + n_row - step, n_row), c, 1 - sub))
    for copy in sends:
        copy.wait_send()
    finish_half(halves - 1)
    matrix_copy.wait()
    for step in range(1, n_row):
        weight(step).wait_send()


def exchange(samples, w, station, taps, sgroup, bgroup, n_row, n_col, n_sub, halves):
    n = n_row * n_col * n_sub
    local, _, chan, frames = samples.shape
    stations = sgroup.shape[1]
    stations2 = 2 * stations
    width = frames // halves
    kqs, block = w.shape
    beams = block // n_row
    any_space = pl.BlockSpec(memory_space=pltpu.HBM)
    vmem = pl.BlockSpec(memory_space=pltpu.VMEM)
    dma = pltpu.SemaphoreType.DMA
    sends = ((n_row - 1) * 3 + 2 + n_row) * halves
    bf16 = jnp.bfloat16
    inputs = (samples, w, station, taps, sgroup, bgroup)
    return pl.pallas_call(
        functools.partial(exchange_kernel, n_row, n_col, n_sub),
        out_shape=(
            jax.ShapeDtypeStruct((halves, n, stations2, width), bf16),
            jax.ShapeDtypeStruct((beams * 2 * chan, chan * stations2), bf16),
        ),
        in_specs=[any_space] * 6,
        out_specs=(vmem, any_space),
        scratch_shapes=[pltpu.VMEM((beams * 2 * chan, chan * stations2), bf16)]
        + [pltpu.VMEM(a.shape, a.dtype) for a in inputs]
        + [
            pltpu.VMEM((chan, halves, 2, local, width), bf16),
            pltpu.VMEM((halves, 2, n, local, width), bf16),
            pltpu.VMEM((n_row, beams, kqs), bf16),
            pltpu.VMEM((n_row, beams, kqs), bf16),
            pltpu.VMEM((beams, chan * stations2), jnp.float32),
            pltpu.VMEM((beams, chan * stations2), jnp.float32),
            dma((len(inputs),)), dma((2,)), dma((halves, n)), dma((halves, n)),
            dma((n_row,)), dma((n_row,)), dma((sends,)), dma((halves, n)),
        ],
        compiler_params=pltpu.CompilerParams(
            collective_id=0, has_side_effects=True, vmem_limit_bytes=56 * 1024 * 1024
        ),
        name="exchange",
    )(*inputs)


def fourier(points):
    count = len(points)
    if count == 1:
        return points
    even, odd = fourier(points[0::2]), fourier(points[1::2])
    half = count // 2
    low, high = [], []
    for index in range(half):
        (er, ei), (r, i) = even[index], odd[index]
        if index == 0:
            tr, ti = r, i
        elif 4 * index == count:
            tr, ti = i, -r
        else:
            c, s = math.cos(2 * math.pi * index / count), math.sin(2 * math.pi * index / count)
            if 8 * index == count:
                tr, ti = (r + i) * c, (i - r) * c
            elif 8 * index == 3 * count:
                tr, ti = (i - r) * s, -(r + i) * s
            else:
                tr, ti = r * c + i * s, i * c - r * s
        low.append((er + tr, ei + ti))
        high.append((er - tr, ei - ti))
    return low + high

def beam_kernel(
    lanes_ref, matrix_ref, taps_ref, vis_ref, out_ref,
    spectra, gram, inverse_ref, wide_taps,
):
    halves, chan, stations2, width = lanes_ref.shape
    stations = stations2 // 2
    frames = halves * width
    step_index = pl.program_id(0)
    size = out_ref.shape[0]

    def product():
        return jnp.dot(
            matrix_ref[...],
            spectra[...].reshape(chan * stations2, frames),
            preferred_element_type=jnp.float32,
        )

    @pl.when(step_index == 0)
    def _():
        step_rows = 16

        @pl.loop(0, stations // step_rows)
        def _(block):
            low = pl.multiple_of(block * step_rows, step_rows)
            for start in range(0, frames, 128):
                h, inner = divmod(start, width)
                points = [
                    tuple(
                        lanes_ref[
                            h, c, pl.ds(low + q * stations, step_rows), inner : inner + 128
                        ].astype(jnp.float32)
                        for q in range(2)
                    )
                    for c in range(chan)
                ]
                for k, parts in enumerate(fourier(points)):
                    for q, value in enumerate(parts):
                        spectra[
                            k, pl.ds(low + q * stations, step_rows), start : start + 128
                        ] = value.astype(jnp.bfloat16)

        chan_rows, _, own, _ = vis_ref.shape
        first = lax.axis_index("row") * chan_rows
        block_index = lax.axis_index(("col", "sub"))
        begin = pl.multiple_of(block_index * own, own)
        for k in range(chan_rows):
            block = spectra[first + k]
            gram[k] = lax.dot_general(
                block, block, (((1,), (1,)), ((), ())), preferred_element_type=jnp.float32
            )
            top = gram[k, pl.ds(begin, own), :]
            bottom = gram[k, pl.ds(begin + stations, own), :]
            vis_ref[k, 0] = (top[:, :stations] + bottom[:, stations:]) * (1.0 / frames)
            vis_ref[k, 1] = (bottom[:, :stations] - top[:, stations:]) * (1.0 / frames)

        for tap in range(taps_ref.shape[0]):
            there = lax.broadcasted_iota(jnp.int32, (chan, chan), 1)
            here = lax.broadcasted_iota(jnp.int32, (chan, chan), 0)
            values = jnp.where(there == here, taps_ref[tap : tap + 1, :], 0.0)
            wide_taps[tap] = jnp.broadcast_to(
                jnp.sum(values, axis=1, keepdims=True), (chan, 128)
            )

    lane = lax.broadcasted_iota(jnp.int32, (8, 128), 1)
    later = [None] + [lane >= amount for amount in range(1, taps_ref.shape[0])]

    def shift(tiles, amount):
        turned = [pltpu.roll(tile, amount, 1) for tile in tiles]
        before = [jnp.zeros_like(turned[0])] + turned[:-1]
        return [jnp.where(later[amount], t, b) for t, b in zip(turned, before)]

    taps = taps_ref.shape[0]
    stride = 4
    starts = range(0, frames, 128)

    inverse_ref[...] = product()
    for top in range(0, chan, 8):
        tap_tiles = [wide_taps[tap, top : top + 8, :] for tap in range(taps)]

        def one(index, carry, top=top, tap_tiles=tap_tiles):
            at = pl.multiple_of(index * chan + top, 8)
            tiles = [inverse_ref[pl.ds(at, 8), start : start + 128] for start in starts]
            moved = [tiles] + [shift(tiles, amount) for amount in range(1, stride)]
            total_tiles = None
            for high in range(taps // stride - 1, -1, -1):
                if total_tiles is not None:
                    total_tiles = shift(total_tiles, stride)
                for low in range(stride):
                    tap = tap_tiles[high * stride + low]
                    terms = [tap * tile for tile in moved[low]]
                    total_tiles = (
                        terms
                        if total_tiles is None
                        else [a + t for a, t in zip(total_tiles, terms)]
                    )
            for start, tile in zip(starts, total_tiles):
                out_ref[pl.ds(at, 8), start : start + 128] = tile
            return carry

        lax.fori_loop(0, size // chan, one, 0, unroll=16)


def beamform(lanes, matrix, taps, vis_shape, rows):
    halves, chan, stations2, width = lanes.shape
    frames = halves * width
    beams = matrix.shape[0] // (2 * chan)
    whole = lambda *shape: pl.BlockSpec(shape, lambda i: (0,) * len(shape))
    vmem = pl.BlockSpec(memory_space=pltpu.VMEM)
    vis, series = pl.pallas_call(
        beam_kernel,
        grid=(beams // rows,),
        out_shape=(
            jax.ShapeDtypeStruct(vis_shape, jnp.float32),
            jax.ShapeDtypeStruct((matrix.shape[0], frames), jnp.float32),
        ),
        in_specs=[
            whole(*lanes.shape),
            pl.BlockSpec((rows * 2 * chan, matrix.shape[1]), lambda i: (i, 0)),
            whole(*taps.shape),
        ],
        out_specs=(
            whole(*vis_shape),
            pl.BlockSpec((rows * 2 * chan, frames), lambda i: (i, 0)),
        ),
        scratch_shapes=[
            pltpu.VMEM((chan, stations2, frames), jnp.bfloat16),
            pltpu.VMEM((vis_shape[0], stations2, stations2), jnp.float32),
            pltpu.VMEM((rows * 2 * chan, frames), jnp.float32),
            pltpu.VMEM((taps.shape[0], chan, 128), jnp.float32),
        ],
        compiler_params=pltpu.CompilerParams(
            dimension_semantics=("arbitrary",), vmem_limit_bytes=56 * 1024 * 1024
        ),
        name="beamform",
    )(lanes, matrix, taps)
    return vis, series.reshape(beams, 2, chan, frames)


def lane_body(
    samples, analysis_taps, synthesis_taps, antenna_station, station_group, beam_group, beam_weights
):
    n_row, n_col, n_sub = (lax.axis_size(name) for name in ("row", "col", "sub"))
    stations = station_group.shape[0]
    chan_rows, _, block, _ = beam_weights.shape
    w = beam_weights.transpose(0, 1, 3, 2).reshape(chan_rows * 2 * stations, block)
    lanes, matrix = exchange(
        samples, w, antenna_station.reshape(1, -1), analysis_taps,
        station_group.reshape(1, -1), beam_group.reshape(-1, 128), n_row, n_col, n_sub, 2,
    )
    tile_rows = stations // (n_col * n_sub)
    return beamform(lanes, matrix, synthesis_taps, (chan_rows, 2, tile_rows, stations), 8)


def solution(mesh):
    shape = mesh.shape
    fits = (
        shape["row"] * shape["col"] * shape["sub"] == 16 and shape["col"] == 2 and shape["sub"] == 2
    )
    return jax.shard_map(
        lane_body if fits else body,
        mesh=mesh,
        in_specs=(
            P(("grp", "row", "col", "sub"), None, None, None),
            P(),
            P(),
            P("grp"),
            P("grp", None),
            P("grp"),
            P(("grp", "row"), None, ("col", "sub"), None),
        ),
        out_specs=(
            P("row", None, ("grp", "col", "sub"), None),
            P(("grp", "col", "sub", "row"), None, None, None),
        ),
        check_vma=False,
    )
```
